256 devices in a mesh: grp: 4 (over x), seq: 16 (over z, core), mp: 4 (over y).
Axes of the slice: x: 4, y: 4, z: 8, core: 2. Of those that a mesh axis runs over, the one named last changes fastest.
Arguments:
- dec_query: bfloat16 [4, 4096, 4096], P('grp', 'seq', 'mp'), may hold values from -6 to 6
- dec_key: bfloat16 [4, 4096, 4096], P('grp', 'seq', 'mp'), may hold values from -6 to 6
- dec_value: bfloat16 [4, 4096, 4096], P('grp', 'seq', 'mp'), may hold values from -6 to 6
- cross_query: bfloat16 [4, 4096, 4096], P('grp', 'seq', 'mp'), may hold values from -6 to 6
- enc_query: bfloat16 [512, 128, 4096], P(('grp', 'seq', 'mp')), may hold values from -6 to 6
- enc_key: bfloat16 [512, 128, 4096], P(('grp', 'seq', 'mp')), may hold values from -6 to 6
- enc_value: bfloat16 [512, 128, 4096], P(('grp', 'seq', 'mp')), may hold values from -6 to 6
- nbr_index: int32 [4, 64, 2], P('grp', 'seq'), may hold values from 0 to 511, as said below
- seq_lengths: int32 [4], P('grp'), may hold values from 1024 to 4096, as said below
Outputs:
- self_attended: bfloat16 [4, 4096, 4096], P('grp', 'seq', 'mp')
- cross_attended: bfloat16 [4, 4096, 4096], P('grp', 'seq', 'mp')
The draws below stay inside these ranges and needn't reach their ends.
Inputs may be any that keep to these rules, and one draw needn't show every extreme that they name: `nbr_index`: for the spans of candidate c on seq block s (spans s * 4 to s * 4 + 3), every id n has (n // 8) % 16 == s; among these 8 ids at most 4 share the value n // 128, and one value is shared by exactly 4; the two ids of a span differ. `seq_lengths`: some candidate has exactly 4096 valid tokens.
All inputs are finite; a program needn't handle non-finite values.
Results may differ from the reference program's by a relative error of at most 0.017.
Values may be sent and summed in bfloat16 or wider, within the bound.
A program may use at most 192 MiB of HBM per device.

```python
from functools import partial
import jax
import jax.numpy as jnp
from jax import lax

HEADS = 32
HS = 128
SPAN = 64
NBR_LEN = 128
NEIGH_K = 2
SPAN_DEV = 4
NB_DEV = 2
CANDS = 4
HD = 4096
NCHUNK = 64
LENGTH = 4096
STORE = 512
CAP = 4
N_GRP = 4
N_SEQ = 16
N_MP = 4


def drawn_values(key, shape):
    return jnp.clip(jax.random.normal(key, shape, jnp.float32), -6.0, 6.0)


def draw_dec_query(key, part):
    key = jax.random.fold_in(key, 1)
    shape = (CANDS, LENGTH, HD)
    values = drawn_values(key, shape)
    return values.astype(jnp.bfloat16)


def draw_dec_key(key, part):
    key = jax.random.fold_in(key, 2)
    shape = (CANDS, LENGTH, HD)
    values = drawn_values(key, shape)
    return values.astype(jnp.bfloat16)


def draw_cross_query(key, part):
    key = jax.random.fold_in(key, 3)
    shape = (CANDS, LENGTH, HD)
    values = drawn_values(key, shape)
    return values.astype(jnp.bfloat16)


def draw_enc_query(key, part):
    key = jax.random.fold_in(key, 4)
    shape = (STORE, NBR_LEN, HD)
    values = drawn_values(key, shape)
    return values.astype(jnp.bfloat16)


def draw_enc_key(key, part):
    key = jax.random.fold_in(key, 5)
    shape = (STORE, NBR_LEN, HD)
    values = drawn_values(key, shape)
    return values.astype(jnp.bfloat16)


def draw_seq_lengths(key, part):
    key = jax.random.fold_in(key, 8)
    drawn = jax.random.randint(jax.random.fold_in(key, 1), (CANDS,), LENGTH // 4, LENGTH + 1)
    longest = jax.random.randint(jax.random.fold_in(key, 2), (), 0, CANDS)
    return jnp.where(jnp.arange(CANDS) == longest, LENGTH, drawn).astype(jnp.int32)


def draw_nbr_index(key, part):
    key = jax.random.fold_in(key, 11)
    request_count = SPAN_DEV * NEIGH_K
    pool_size = N_MP * NB_DEV
    cand_ids = jnp.arange(CANDS, dtype=jnp.int32)[:, None, None]
    first_group = jax.random.randint(jax.random.fold_in(key, 1), (CANDS, N_SEQ, 1), 0, N_GRP)
    first_group = jnp.where(cand_ids == 0, N_GRP - 1, jnp.where(cand_ids == 1, 0, first_group))
    straight = jnp.broadcast_to(jnp.arange(request_count, dtype=jnp.int32), (CANDS, N_SEQ, request_count))
    ordering = jax.random.permutation(jax.random.fold_in(key, 2), straight, axis=2, independent=True)
    ordering = jnp.where(cand_ids < 2, straight, ordering)
    other_group = (first_group + 1 + jax.random.randint(jax.random.fold_in(key, 3), (CANDS, N_SEQ, request_count), 0, N_GRP - 1)) % N_GRP
    target = jnp.where(ordering < CAP, first_group, other_group)
    base_ids = jax.random.randint(jax.random.fold_in(key, 4), (CANDS, N_SEQ, SPAN_DEV, 1), 0, pool_size)
    cand_four = jnp.arange(CANDS, dtype=jnp.int32)[:, None, None, None]
    span_four = jnp.arange(SPAN_DEV, dtype=jnp.int32)[None, None, :, None]
    base_ids = jnp.where((cand_four == 0) & (span_four == 0), pool_size - 1, base_ids)
    base_ids = jnp.where((cand_four == 1) & (span_four == 0), 0, base_ids)
    step_ids = 1 + jax.random.randint(jax.random.fold_in(key, 5), (CANDS, N_SEQ, SPAN_DEV, 1), 0, pool_size - 1)
    second = jnp.arange(NEIGH_K, dtype=jnp.int32)[None, None, None, :] == 1
    local_ids = (base_ids + jnp.where(second, step_ids, 0)) % pool_size
    local_ids = local_ids.reshape(CANDS, N_SEQ, request_count)
    seq_ids = jnp.arange(N_SEQ, dtype=jnp.int32)[None, :, None]
    result = (target * N_SEQ + seq_ids) * pool_size + local_ids
    return result.reshape(CANDS, NCHUNK, NEIGH_K).astype(jnp.int32)


def shard_levels(key, extent, pieces, smallest, largest):
    level, own = 1.0, jax.random.fold_in(key, 6)
    for dim, blocks in pieces:
        heights = jnp.exp(jax.random.uniform(jax.random.fold_in(own, dim), (blocks,), jnp.float32, smallest / len(pieces), largest / len(pieces)))
        level = level * jnp.repeat(heights, extent[dim] // blocks).reshape([-1 if axis == dim else 1 for axis in range(len(extent))])
    return level


def scatter_about(own_key, extent, deviation, limit, cuts=(), held_as=jnp.bfloat16):
    values = deviation * jax.random.normal(own_key, extent, jnp.float32)
    if cuts:
        values = values * shard_levels(own_key, extent, cuts, -0.22, 0.18)
    return jnp.clip(values, -limit, limit).astype(held_as)


def setup_inputs(seed: int = 0) -> dict:
    splits = jax.random.split(jax.random.key(seed), 10)
    return {
        "dec_query": draw_dec_query(jax.random.fold_in(splits[9], 71), 0),
        "dec_key": draw_dec_key(jax.random.fold_in(splits[9], 71), 0),
        "dec_value": scatter_about(splits[2], (CANDS, LENGTH, HD), 1.0, 6.0, ((0, 4), (1, 16), (2, 4))),
        "cross_query": draw_cross_query(jax.random.fold_in(splits[9], 71), 0),
        "enc_query": draw_enc_query(jax.random.fold_in(splits[9], 71), 0),
        "enc_key": draw_enc_key(jax.random.fold_in(splits[9], 71), 0),
        "enc_value": scatter_about(splits[6], (STORE, NBR_LEN, HD), 1.0, 6.0, ((0, 256),)),
        "nbr_index": draw_nbr_index(jax.random.fold_in(splits[9], 71), 0),
        "seq_lengths": draw_seq_lengths(jax.random.fold_in(splits[9], 71), 0),
    }


MASKED = -1e30


def attend(query_rows, key_rows, value_rows, allowed):
    scores = jnp.einsum("qhd,khd->hqk", query_rows.astype(jnp.float32), key_rows.astype(jnp.float32)) * (HS ** -0.5)
    scores = jnp.where(allowed[None], scores, MASKED)
    row_top = jnp.max(scores, axis=2, keepdims=True)
    weights = jnp.where(allowed[None], jnp.exp(scores - row_top), 0.0).astype(jnp.bfloat16)
    row_total = jnp.sum(weights.astype(jnp.float32), axis=2)
    blended = jnp.einsum("hqk,khd->qhd", weights.astype(jnp.float32), value_rows.astype(jnp.float32))
    return blended / jnp.transpose(row_total)[:, :, None]


def encode_one(packed):
    queries, keys_in, values_in = packed
    shape_heads = (NBR_LEN, HEADS, HS)
    allowed = jnp.ones((NBR_LEN, NBR_LEN), dtype=bool)
    blended = attend(queries.reshape(shape_heads), keys_in.reshape(shape_heads), values_in.reshape(shape_heads), allowed)
    blended = blended.reshape(NBR_LEN, HD)
    new_keys = (keys_in.astype(jnp.float32) + blended).astype(jnp.bfloat16)
    new_values = (values_in.astype(jnp.float32) + blended).astype(jnp.bfloat16)
    return new_keys, new_values


def self_candidate(packed):
    queries, keys_in, values_in, seq_length = packed
    shape_heads = (LENGTH, HEADS, HS)
    key_heads = keys_in.reshape(shape_heads)
    value_heads = values_in.reshape(shape_heads)
    block_rows = LENGTH // N_SEQ
    key_pos = jnp.arange(LENGTH, dtype=jnp.int32)

    def per_block(block_start):
        query_rows = lax.dynamic_slice_in_dim(queries, block_start, block_rows, 0).reshape(block_rows, HEADS, HS)
        query_pos = block_start + jnp.arange(block_rows, dtype=jnp.int32)
        allowed = (key_pos[None, :] <= query_pos[:, None]) & (key_pos[None, :] < seq_length)
        return attend(query_rows, key_heads, value_heads, allowed).reshape(block_rows, HD)

    starts = jnp.arange(N_SEQ, dtype=jnp.int32) * block_rows
    result = lax.map(per_block, starts).reshape(LENGTH, HD)
    live_rows = (key_pos < seq_length)[:, None]
    return jnp.where(live_rows, result, 0.0).astype(jnp.bfloat16)


def cross_candidate(packed, nbr_keys, nbr_values):
    queries, span_ids, seq_length = packed
    padded = jnp.concatenate([jnp.zeros((1, HD), queries.dtype), queries, jnp.zeros((SPAN - 1, HD), queries.dtype)], axis=0)
    grouped = padded[SPAN:].reshape(NCHUNK, SPAN, HEADS, HS)
    allowed = jnp.ones((SPAN, NEIGH_K * NBR_LEN), dtype=bool)

    def per_span(inner):
        query_rows, neighbour_ids = inner
        key_rows = nbr_keys[neighbour_ids].reshape(NEIGH_K * NBR_LEN, HEADS, HS)
        value_rows = nbr_values[neighbour_ids].reshape(NEIGH_K * NBR_LEN, HEADS, HS)
        return attend(query_rows, key_rows, value_rows, allowed).reshape(SPAN, HD)

    result = lax.map(per_span, (grouped, span_ids)).reshape(LENGTH, HD)
    shifted = jnp.concatenate([jnp.zeros((SPAN - 1, HD), result.dtype), result[:LENGTH - SPAN + 1]], axis=0)
    position = jnp.arange(LENGTH, dtype=jnp.int32)
    live_rows = ((position >= SPAN - 1) & (position < seq_length))[:, None]
    return jnp.where(live_rows, shifted, 0.0).astype(jnp.bfloat16)


def reference(dec_query, dec_key, dec_value, cross_query, enc_query, enc_key, enc_value, nbr_index, seq_lengths):
    nbr_keys, nbr_values = lax.map(encode_one, (enc_query, enc_key, enc_value))
    self_attended = lax.map(self_candidate, (dec_query, dec_key, dec_value, seq_lengths))
    cross_attended = lax.map(partial(cross_candidate, nbr_keys=nbr_keys, nbr_values=nbr_values), (cross_query, nbr_index, seq_lengths))
    return (self_attended, cross_attended)
```

```python
import functools
import math

import jax
import jax.numpy as jnp
from jax import lax
from jax.experimental import pallas as pl
from jax.experimental.pallas import tpu as pltpu
from jax.sharding import PartitionSpec as P

HS = 128
SPAN = 64
CAP = 4
CHUNKS = 4
PAIR = 2 * HS
ROWS = 256
WIDTH = 1024
SCALE = HS ** (-0.5) * math.log2(math.e)
MASKED = -1e30
MESH = pl.DeviceIdType.MESH
F32 = jnp.float32
BF16 = jnp.bfloat16
NT = (((1,), (1,)), ((), ()))


def mod(a, n):
    return lax.rem(a, n)


def scores_of(q, k):
    return lax.dot_general(q, k, NT, preferred_element_type=F32)


def mix(weights, v):
    return jnp.dot(weights.astype(BF16), v, preferred_element_type=F32)


def kernel(
    nbr, lens, dq, dk, dv, cq, eq, ek, ev,
    self_out, cross_out,
    eqv, ekv, evv, cqv, halo, qf,
    kvs0, kvs1, kvs2, kvs3,
    pool0, pool1, pool2, pool3,
    qb0, qb1, qb2, qb3,
    os0, os1, os2, os3,
    ss0, ss1, ss2, ss3,
    stage, o_in, st_in, stat, of, tail_s, tail_in, co,
    qs, kf, vf, os_self,
    idx_s, idx_all, idx_sm, row_tab, id_tab, req_tab,
    load_sem, z_send, z_recv, f_send, f_recv, y_send, y_recv, y_loc,
    q_send, q_recv, o_send, o_recv, t_send, t_recv, i_send, i_recv,
    b_send, b_recv, h_send, h_recv, misc,
):
    kvs = (kvs0, kvs1, kvs2, kvs3)
    pool = (pool0, pool1, pool2, pool3)
    qb = (qb0, qb1, qb2, qb3)
    os = (os0, os1, os2, os3)
    ss = (ss0, ss1, ss2, ss3)
    g = lax.axis_index("grp")
    s = lax.axis_index("seq")
    m = lax.axis_index("mp")
    z = lax.div(s, 2)
    core = lax.rem(s, 2)
    seq_len = lens[0]

    def z_dev(zz):
        return (g, 2 * zz + core, m)

    def y_dev(mm):
        return (g, s, mm)

    def x_dev(gg):
        return (gg, s, m)

    partner = (g, s + 1 - 2 * core, m)
    other = (g, mod(s + 15 + 2 * core, 16), m)
    behind = (g, mod(s + 15, 16), m)
    ahead = (g, mod(s + 1, 16), m)

    def remote(src, dst, send, recv, dev):
        return pltpu.make_async_remote_copy(
            src_ref=src, dst_ref=dst, send_sem=send, recv_sem=recv,
            device_id=dev, device_id_type=MESH,
        )

    loads = [
        pltpu.make_async_copy(src, dst, load_sem.at[n])
        for n, (src, dst) in enumerate(((cq.at[0], cqv), (eq, eqv), (ek, ekv), (ev, evv)))
    ]
    for c in loads:
        c.start()
    own = pl.ds(pl.multiple_of(z * HS, HS), HS)
    local_in = [
        pltpu.make_async_copy(dq.at[0, :, own], qs.at[z], load_sem.at[4]),
        pltpu.make_async_copy(dk.at[0, :, own], kf.at[s], load_sem.at[5]),
        pltpu.make_async_copy(dv.at[0, :, own], vf.at[s], load_sem.at[6]),
    ]
    for c in local_in:
        c.start()

    bar = pltpu.get_barrier_semaphore()
    peers = [z_dev(mod(z + off, 8)) for off in range(1, 8)]
    peers += [y_dev(mod(m + off, 4)) for off in range(1, 4)]
    peers += [x_dev(mod(g + off, 4)) for off in range(1, 4)]
    peers += [partner, other]
    for dev in peers:
        pl.semaphore_signal(bar, inc=1, device_id=dev, device_id_type=MESH)
    pl.semaphore_wait(bar, len(peers))

    halo_copy = remote(cq.at[0, pl.ds(0, SPAN)], halo, h_send.at[0], h_recv.at[0], behind)
    halo_copy.start()

    lane8 = lax.broadcasted_iota(jnp.int32, (8, 128), 1)
    packed = jnp.zeros((8, 128), jnp.int32)
    for n in range(8):
        packed = jnp.where(lane8 == n, nbr[0, n // 2, n % 2], packed)
    idx_s[...] = packed
    idx_copies = [
        remote(idx_s, idx_all.at[g], i_send.at[off - 1], i_recv.at[off - 1], x_dev(mod(g + off, 4)))
        for off in range(1, 4)
    ]
    for c in idx_copies:
        c.start()
    idx_local = pltpu.make_async_copy(idx_s, idx_all.at[g], misc.at[0])
    idx_local.start()

    z_order = (4, 3, 5, 2, 6, 1, 7)

    def z_copies(off):
        zz = mod(z + off, 8)
        cols = pl.ds(pl.multiple_of(zz * HS, HS), HS)
        dev = z_dev(zz)
        n = (off - 1) * 3
        return (
            remote(dk.at[0, :, cols], kf.at[s], z_send.at[n], z_recv.at[n], dev),
            remote(dq.at[0, :, cols], qs.at[z], z_send.at[n + 1], z_recv.at[n + 1], dev),
            remote(dv.at[0, :, cols], vf.at[s], z_send.at[n + 2], z_recv.at[n + 2], dev),
        )

    def z_arrivals(off):
        zz = mod(z + 8 - off, 8)
        n = (off - 1) * 3
        dev = z_dev(zz)
        b = 2 * zz + core
        return (
            remote(kf.at[b], kf.at[b], z_send.at[n], z_recv.at[n], dev),
            remote(qs.at[zz], qs.at[zz], z_send.at[n + 1], z_recv.at[n + 1], dev),
            remote(vf.at[b], vf.at[b], z_send.at[n + 2], z_recv.at[n + 2], dev),
        )

    def forwards(off):
        b = 2 * mod(z + 8 - off, 8) + core
        n = off * 2
        return (
            remote(kf.at[b], kf.at[b], f_send.at[n], f_recv.at[n], partner),
            remote(vf.at[b], vf.at[b], f_send.at[n + 1], f_recv.at[n + 1], partner),
        )

    def forward_arrivals(off):
        b = 2 * mod(z + 8 - off, 8) + 1 - core
        n = off * 2
        return (
            remote(kf.at[b], kf.at[b], f_send.at[n], f_recv.at[n], partner),
            remote(vf.at[b], vf.at[b], f_send.at[n + 1], f_recv.at[n + 1], partner),
        )

    for part in range(3):
        for off in z_order:
            z_copies(off)[part].start()

    def y_copy(hc, off):
        return remote(
            kvs[hc].at[off], pool[hc].at[pl.ds(2 * m, 2)],
            y_send.at[hc * 3 + off], y_recv.at[hc * 3 + off], y_dev(mod(m + 1 + off, 4)),
        )

    def y_arrival(hc, off):
        mm = mod(m + 3 - off, 4)
        return remote(
            kvs[hc].at[off], pool[hc].at[pl.ds(2 * mm, 2)],
            y_send.at[hc * 3 + off], y_recv.at[hc * 3 + off], y_dev(mm),
        )

    def y_local(hc):
        return pltpu.make_async_copy(kvs[hc].at[3], pool[hc].at[pl.ds(2 * m, 2)], y_loc.at[hc])

    def encode(hc):
        out = kvs[hc]

        def step(off, carry):
            t = mod(m + 1 + off, 4)
            for n in range(2):
                for j in range(2):
                    cols = pl.ds(pl.multiple_of((t * 8 + hc * 2 + j) * HS, HS), HS)
                    q, k, v = eqv[n, :, cols], ekv[n, :, cols], evv[n, :, cols]
                    sc = scores_of(q, k)
                    top = jnp.max(sc, axis=1, keepdims=True)
                    w = jnp.exp2((sc - top) * SCALE)
                    inv = 1.0 / jnp.sum(w, axis=1, keepdims=True)
                    mixed = mix(w, v) * inv
                    at = slice(j * HS, (j + 1) * HS)
                    out[off, n, 0, :, at] = (k.astype(F32) + mixed).astype(BF16)
                    out[off, n, 1, :, at] = (v.astype(F32) + mixed).astype(BF16)

            @pl.when(off < 3)
            def _():
                y_copy(hc, off).start()

            @pl.when(off == 3)
            def _():
                y_local(hc).start()

            return carry

        lax.fori_loop(0, 4, step, 0)

    def q_copy(hc, off):
        mine = qb[hc].at[pl.ds(4 * g, 4)]
        return remote(
            mine, mine, q_send.at[hc * 3 + off], q_recv.at[hc * 3 + off], x_dev(mod(g + 1 + off, 4))
        )

    def q_arrival(hc, off):
        gg = mod(g + 3 - off, 4)
        theirs = qb[hc].at[pl.ds(4 * gg, 4)]
        return remote(
            theirs, theirs, q_send.at[hc * 3 + off], q_recv.at[hc * 3 + off], x_dev(gg)
        )

    def shift_queries():
        loads[0].wait()
        halo_copy.wait_recv()
        qf[0:ROWS, :] = cqv[...].astype(F32)
        qf[ROWS : ROWS + SPAN, :] = halo[...].astype(F32)
        for hc in range(CHUNKS):
            for u in range(4):
                first = SPAN - 1 + SPAN * u
                qb[hc][4 * g + u] = qf[first : first + SPAN, hc * PAIR : (hc + 1) * PAIR].astype(BF16)
            for off in range(3):
                q_copy(hc, off).start()

    def tables():
        for off in range(1, 4):
            gg = mod(g + 4 - off, 4)
            remote(
                idx_s, idx_all.at[gg], i_send.at[off - 1], i_recv.at[off - 1], x_dev(gg)
            ).wait_recv()
        idx_local.wait()
        to_smem = pltpu.make_async_copy(idx_all, idx_sm, misc.at[1])
        to_smem.start()
        to_smem.wait()

        def per_candidate(c, carry):
            ids = [idx_sm[c, 0, n] for n in range(8)]
            count = jnp.int32(0)
            rows = [c * 4] * CAP
            locals_ = [jnp.int32(0)] * CAP
            for n in range(8):
                mine = lax.shift_right_logical(ids[n], 7) == g
                for r in range(CAP):
                    hit = jnp.logical_and(mine, count == r)
                    rows[r] = jnp.where(hit, c * 4 + n // 2, rows[r])
                    locals_[r] = jnp.where(hit, ids[n] & 7, locals_[r])
                count = count + jnp.where(mine, 1, 0)
            for r in range(CAP):
                row_tab[c * 4 + r] = rows[r]
                id_tab[c * 4 + r] = locals_[r]
            return carry

        lax.fori_loop(0, 4, per_candidate, 0)
        targets = [lax.shift_right_logical(nbr[0, n // 2, n % 2], 7) for n in range(8)]
        for n in range(8):
            rank = jnp.int32(0)
            for e in range(n):
                rank = rank + jnp.where(targets[e] == targets[n], 1, 0)
            req_tab[n] = targets[n] * CAP + rank

    lane64 = lax.broadcasted_iota(jnp.int32, (SPAN, 128), 1)

    def o_copy(hc, off):
        return remote(
            os[hc].at[off], o_in.at[pl.ds(4 * g, 4), :, pl.ds(hc * PAIR, PAIR)],
            o_send.at[hc * 3 + off], o_recv.at[hc * 3 + off], x_dev(mod(g + 1 + off, 4)),
        )

    def t_copy(hc, off):
        return remote(
            ss[hc].at[off], st_in.at[4 * g + hc],
            t_send.at[hc * 3 + off], t_recv.at[hc * 3 + off], x_dev(mod(g + 1 + off, 4)),
        )

    def o_local(hc):
        return (
            pltpu.make_async_copy(
                os[hc].at[3], o_in.at[pl.ds(4 * g, 4), :, pl.ds(hc * PAIR, PAIR)], misc.at[2 + hc]
            ),
            pltpu.make_async_copy(ss[hc].at[3], st_in.at[4 * g + hc], misc.at[6 + hc]),
        )

    def cross(hc):
        for off in range(3):
            y_arrival(hc, off).wait_recv()
            q_arrival(hc, off).wait_recv()
        y_local(hc).wait()

        def step(off, carry):
            c = mod(g + 1 + off, 4)
            for r in range(CAP):
                row = row_tab[c * 4 + r]
                local = id_tab[c * 4 + r]
                q2 = qb[hc][row]
                k2 = pool[hc][local, 0]
                v2 = pool[hc][local, 1]
                logs = []
                for j in range(2):
                    at = slice(j * HS, (j + 1) * HS)
                    sc = scores_of(q2[:, at], k2[:, at])
                    top = jnp.max(sc, axis=1, keepdims=True)
                    w = jnp.exp2((sc - top) * SCALE)
                    total = jnp.sum(w, axis=1, keepdims=True)
                    os[hc][off, r, :, at] = (mix(w, v2[:, at]) * (1.0 / total)).astype(BF16)
                    logs.append(top * SCALE + jnp.log2(total))
                stage[r * SPAN : (r + 1) * SPAN, :] = jnp.where(
                    lane64 == 0, logs[0], jnp.where(lane64 == 1, logs[1], 0.0)
                )
            ss[hc][off] = jnp.transpose(stage[...])[0:8]

            @pl.when(off < 3)
            def _():
                o_copy(hc, off).start()
                t_copy(hc, off).start()

            @pl.when(off == 3)
            def _():
                for c_ in o_local(hc):
                    c_.start()

            return carry

        lax.fori_loop(0, 4, step, 0)

    def b_copy(i, k):
        return remote(
            os_self.at[i], self_out.at[0, :, own], b_send.at[k], b_recv.at[k], z_dev(i)
        )

    KEYS = 512
    key_iota = lax.broadcasted_iota(jnp.int32, (ROWS, KEYS), 1)
    row_iota = lax.broadcasted_iota(jnp.int32, (ROWS, KEYS), 0)

    def self_attend():
        def block(k, carry):
            i = mod(z + 1 + k, 8)
            q = qs[i]

            def keys_of(ref, j):
                return ref[pl.ds(2 * j, 2)].reshape(KEYS, HS)

            sc = scores_of(q, keys_of(kf, i))
            sc = jnp.where(key_iota <= row_iota + core * ROWS, sc, MASKED)
            top = jnp.max(sc, axis=1, keepdims=True)
            w = jnp.exp2((sc - top) * SCALE)
            total = jnp.sum(w, axis=1, keepdims=True)
            acc = mix(w, keys_of(vf, i))

            def step(j, state):
                top, total, acc = state
                sc = scores_of(q, keys_of(kf, j))
                new = jnp.maximum(top, jnp.max(sc, axis=1, keepdims=True))
                old = jnp.exp2((top - new) * SCALE)
                w = jnp.exp2((sc - new) * SCALE)
                total = total * old + jnp.sum(w, axis=1, keepdims=True)
                acc = acc * old + mix(w, keys_of(vf, j))
                return new, total, acc

            top, total, acc = lax.fori_loop(0, i, step, (top, total, acc))
            pos = (2 * i + core) * ROWS + lax.broadcasted_iota(jnp.int32, (ROWS, HS), 0)
            os_self[i] = jnp.where(pos < seq_len, acc * (1.0 / total), 0.0).astype(BF16)

            @pl.when(k < 7)
            def _():
                b_copy(i, k).start()

            @pl.when(k == 7)
            def _():
                pltpu.make_async_copy(os_self.at[z], self_out.at[0, :, own], misc.at[10]).start()

            return carry

        lax.fori_loop(0, 8, block, 0)

    own_fwd = forwards(0)
    for c in loads[1:]:
        c.wait()
    encode(0)
    shift_queries()
    encode(1)
    for c in local_in:
        c.wait()
    for c in own_fwd:
        c.start()
    tables()
    encode(2)
    encode(3)
    cross(0)
    cross(1)
    for part in range(3):
        for off in z_order:
            z_arrivals(off)[part].wait_recv()
            if part == 0:
                forwards(off)[0].start()
            if part == 2:
                forwards(off)[1].start()
    cross(2)
    for off in range(8):
        for c in forward_arrivals(off):
            c.wait_recv()
    self_attend()
    cross(3)

    for hc in range(CHUNKS):
        for off in range(3):
            gg = mod(g + 3 - off, 4)
            remote(
                os[hc].at[off], o_in.at[pl.ds(4 * gg, 4), :, pl.ds(hc * PAIR, PAIR)],
                o_send.at[hc * 3 + off], o_recv.at[hc * 3 + off], x_dev(gg),
            ).wait_recv()
            remote(
                ss[hc].at[off], st_in.at[4 * gg + hc],
                t_send.at[hc * 3 + off], t_recv.at[hc * 3 + off], x_dev(gg),
            ).wait_recv()
        for c in o_local(hc):
            c.wait()
    turned = jnp.transpose(st_in[...].reshape(128, 256))
    for gg in range(4):
        part = turned if gg == 0 else pltpu.roll(turned, 128 - 32 * gg, 1)
        for r in range(CAP):
            stat[gg * CAP + r] = part[r * SPAN : (r + 1) * SPAN, :]
    of[ROWS + 56 : ROWS + 64, :] = jnp.zeros((8, WIDTH), F32)

    def combine(u):
        s0, s1 = req_tab[2 * u], req_tab[2 * u + 1]
        l0, l1 = stat[s0], stat[s1]
        top = jnp.maximum(l0, l1)
        w0, w1 = jnp.exp2(l0 - top), jnp.exp2(l1 - top)
        inv = 1.0 / (w0 + w1)
        w0, w1 = w0 * inv, w1 * inv
        o0, o1 = o_in[s0], o_in[s1]
        first = SPAN - 1 + SPAN * u
        for h in range(8):
            lane = (h // 2) * 8 + h % 2
            at = slice(h * HS, (h + 1) * HS)
            of[first : first + SPAN, at] = (
                o0[:, at].astype(F32) * w0[:, lane : lane + 1]
                + o1[:, at].astype(F32) * w1[:, lane : lane + 1]
            )

    combine(3)
    tail_s[...] = of[ROWS : ROWS + SPAN, :].astype(BF16)
    tail_copy = remote(tail_s, tail_in, h_send.at[1], h_recv.at[1], ahead)
    tail_copy.start()
    for u in range(3):
        combine(u)
    first_pos = s * ROWS

    def live(first, rows):
        pos = first_pos + first + lax.broadcasted_iota(jnp.int32, (rows, WIDTH), 0)
        return jnp.logical_and(pos >= SPAN - 1, pos < seq_len)

    co[SPAN:ROWS, :] = jnp.where(live(SPAN, ROWS - SPAN), of[SPAN:ROWS, :], 0.0).astype(BF16)
    tail_copy.wait_recv()
    row = lax.broadcasted_iota(jnp.int32, (SPAN, WIDTH), 0)
    head = jnp.where(row < SPAN - 1, tail_in[...].astype(F32), of[0:SPAN, :])
    co[0:SPAN, :] = jnp.where(live(0, SPAN), head, 0.0).astype(BF16)
    out_copy = pltpu.make_async_copy(co, cross_out.at[0], misc.at[11])
    out_copy.start()

    pltpu.make_async_copy(os_self.at[z], self_out.at[0, :, own], misc.at[10]).wait()
    for k in range(7):
        src = mod(z + 7 - k, 8)
        cols = pl.ds(pl.multiple_of(src * HS, HS), HS)
        remote(
            os_self.at[z], self_out.at[0, :, cols], b_send.at[k], b_recv.at[k], z_dev(src)
        ).wait_recv()
        b_copy(mod(z + 1 + k, 8), k).wait_send()
    halo_copy.wait_send()
    tail_copy.wait_send()
    for c in idx_copies:
        c.wait_send()
    for off in z_order:
        for c in z_copies(off):
            c.wait_send()
    for off in range(8):
        for c in forwards(off):
            c.wait_send()
    for hc in range(CHUNKS):
        for off in range(3):
            y_copy(hc, off).wait_send()
            q_copy(hc, off).wait_send()
            o_copy(hc, off).wait_send()
            t_copy(hc, off).wait_send()
    out_copy.wait()


def local(*args):
    dec_query, dec_key, dec_value, cross_query, enc_query, enc_key, enc_value, nbr_index, seq_lengths = args
    any_ = pl.BlockSpec(memory_space=pl.ANY)
    smem = pl.BlockSpec(memory_space=pltpu.SMEM)
    V = pltpu.VMEM
    dma = lambda n: pltpu.SemaphoreType.DMA((n,))
    scratch = [V((2, 128, 4096), BF16)] * 3
    scratch += [V((ROWS, WIDTH), BF16), V((SPAN, WIDTH), BF16), V((ROWS + SPAN, WIDTH), F32)]
    scratch += [V((4, 2, 2, 128, PAIR), BF16)] * 4
    scratch += [V((8, 2, 128, PAIR), BF16)] * 4
    scratch += [V((16, SPAN, PAIR), BF16)] * 4
    scratch += [V((4, 4, SPAN, PAIR), BF16)] * 4
    scratch += [V((4, 8, 256), F32)] * 4
    scratch += [
        V((256, 128), F32), V((16, SPAN, WIDTH), BF16), V((16, 8, 256), F32),
        V((16, SPAN, 128), F32), V((ROWS + SPAN, WIDTH), F32),
        V((SPAN, WIDTH), BF16), V((SPAN, WIDTH), BF16), V((ROWS, WIDTH), BF16),
    ]
    scratch += [
        V((8, ROWS, HS), BF16), V((16, ROWS, HS), BF16), V((16, ROWS, HS), BF16), V((8, ROWS, HS), BF16)
    ]
    scratch += [
        V((8, 128), jnp.int32), V((4, 8, 128), jnp.int32), pltpu.SMEM((4, 8, 128), jnp.int32),
        pltpu.SMEM((16,), jnp.int32), pltpu.SMEM((16,), jnp.int32), pltpu.SMEM((8,), jnp.int32),
    ]
    scratch += [dma(n) for n in (7, 21, 21, 16, 16, 12, 12, 4, 12, 12, 12, 12, 12, 12, 3, 3, 7, 7, 2, 2, 12)]
    shape = jax.ShapeDtypeStruct((1, ROWS, WIDTH), BF16)
    return pl.pallas_call(
        kernel,
        out_shape=(shape, shape),
        in_specs=[smem, smem] + [any_] * 7,
        out_specs=(any_, any_),
        scratch_shapes=scratch,
        compiler_params=pltpu.CompilerParams(
            collective_id=0, has_side_effects=True, vmem_limit_bytes=56 << 20
        ),
        name="retro_block",
    )(nbr_index, seq_lengths, dec_query, dec_key, dec_value, cross_query, enc_query, enc_key, enc_value)


def solution(mesh):
    rows = P("grp", "seq", "mp")
    store = P(("grp", "seq", "mp"), None, None)
    return jax.shard_map(
        local,
        mesh=mesh,
        in_specs=(rows, rows, rows, rows, store, store, store, P("grp", "seq", None), P("grp")),
        out_specs=(rows, rows),
        check_vma=False,
    )
```

```python
import functools
import math

import jax
import jax.numpy as jnp
from jax import lax
from jax.experimental import pallas as pl
from jax.experimental.pallas import tpu as pltpu
from jax.sharding import PartitionSpec as P

HS = 128
SPAN = 64
CAP = 4
HEADS_OF = (2, 2, 2, 1, 1)
FIRST = (0, 2, 4, 6, 7)
CHUNKS = len(HEADS_OF)
ROWS = 256
WIDTH = 1024
SCALE = HS ** (-0.5) * math.log2(math.e)
MASKED = -1e30
MESH = pl.DeviceIdType.MESH
F32 = jnp.float32
BF16 = jnp.bfloat16
NT = (((1,), (1,)), ((), ()))


def mod(a, n):
    return lax.rem(a, n)


def scores_of(q, k):
    return lax.dot_general(q, k, NT, preferred_element_type=F32)


def mix(weights, v):
    return jnp.dot(weights.astype(BF16), v, preferred_element_type=F32)


def fold(x, op):
    parts = [x[:, a : a + HS] for a in range(0, x.shape[1], HS)]
    while len(parts) > 1:
        parts = [op(parts[a], parts[a + 1]) for a in range(0, len(parts), 2)]
    return parts[0]


def attend_all(queries, keys, values):
    scores = [scores_of(q, k) for q, k in zip(queries, keys)]
    tops = [jnp.max(x, axis=1, keepdims=True) for x in scores]
    weights = [jnp.exp2((x - top) * SCALE) for x, top in zip(scores, tops)]
    totals = [jnp.sum(w, axis=1, keepdims=True) for w in weights]
    sums = [mix(w, v) for w, v in zip(weights, values)]
    return tops, totals, [x * (1.0 / total) for x, total in zip(sums, totals)]


def kernel(
    nbr, lens, dq, dk, dv, cq, eq, ek, ev,
    self_out, cross_out,
    eqv, ekv, evv, cqv, halo, qf,
    stage, stat, of, co,
    qs, kf, vf, os_self, sc_buf,
    idx_s, idx_all, idx_sm, row_tab, id_tab, req_tab,
    load_sem, z_send, z_recv, f_send, f_recv, y_send, y_recv, y_loc,
    q_send, q_recv, o_send, o_recv, t_send, t_recv, o_loc, t_loc, i_send, i_recv,
    b_send, b_recv, h_send, h_recv, e_send, e_recv, c_sem, misc,
    *chunked,
):
    kvs, pool, qb, os, ss, o_in, st_in, tail_s, tail_in = (
        chunked[n * CHUNKS : (n + 1) * CHUNKS] for n in range(9)
    )
    g = lax.axis_index("grp")
    s = lax.axis_index("seq")
    m = lax.axis_index("mp")
    z = lax.div(s, 2)
    core = lax.rem(s, 2)
    seq_len = lens[0]

    def z_dev(zz):
        return (g, 2 * zz + core, m)

    def y_dev(mm):
        return (g, s, mm)

    def x_dev(gg):
        return (gg, s, m)

    partner = (g, s + 1 - 2 * core, m)
    other = (g, mod(s + 15 + 2 * core, 16), m)
    behind = (g, mod(s + 15, 16), m)
    ahead = (g, mod(s + 1, 16), m)

    def remote(src, dst, send, recv, dev):
        return pltpu.make_async_remote_copy(
            src_ref=src, dst_ref=dst, send_sem=send, recv_sem=recv,
            device_id=dev, device_id_type=MESH,
        )

    loads = [
        pltpu.make_async_copy(src, dst, load_sem.at[n])
        for n, (src, dst) in enumerate(((cq.at[0], cqv), (eq, eqv), (ek, ekv), (ev, evv)))
    ]
    for c in loads:
        c.start()
    own = pl.ds(pl.multiple_of(z * HS, HS), HS)
    local_in = [
        pltpu.make_async_copy(dq.at[0, :, own], qs.at[z], load_sem.at[4]),
        pltpu.make_async_copy(dk.at[0, :, own], kf.at[s], load_sem.at[5]),
        pltpu.make_async_copy(dv.at[0, :, own], vf.at[s], load_sem.at[6]),
    ]
    for c in local_in:
        c.start()

    bar = pltpu.get_barrier_semaphore()
    peers = [z_dev(mod(z + off, 8)) for off in range(1, 8)]
    peers += [y_dev(mod(m + off, 4)) for off in range(1, 4)]
    peers += [x_dev(mod(g + off, 4)) for off in range(1, 4)]
    peers += [partner, other]
    for dev in peers:
        pl.semaphore_signal(bar, inc=1, device_id=dev, device_id_type=MESH)
    pl.semaphore_wait(bar, len(peers))

    halo_copy = remote(cq.at[0, pl.ds(0, SPAN)], halo, h_send.at[0], h_recv.at[0], behind)
    halo_copy.start()

    lane8 = lax.broadcasted_iota(jnp.int32, (8, 128), 1)
    packed = jnp.zeros((8, 128), jnp.int32)
    for n in range(8):
        packed = jnp.where(lane8 == n, nbr[0, n % 2, n // 2], packed)
    idx_s[...] = packed
    idx_copies = [
        remote(idx_s, idx_all.at[g], i_send.at[off - 1], i_recv.at[off - 1], x_dev(mod(g + off, 4)))
        for off in range(1, 4)
    ]
    for c in idx_copies:
        c.start()
    idx_local = pltpu.make_async_copy(idx_s, idx_all.at[g], misc.at[0])
    idx_local.start()

    z_order = (4, 3, 5, 2, 6, 1, 7)

    def z_copy(off, part):
        zz = mod(z + off, 8)
        cols = pl.ds(pl.multiple_of(zz * HS, HS), HS)
        src = (dk, dq, dv)[part].at[0, :, cols]
        dst = (kf.at[s], qs.at[z], vf.at[s])[part]
        n = (off - 1) * 3 + part
        return remote(src, dst, z_send.at[n], z_recv.at[n], z_dev(zz))

    def z_arrival(off, part):
        zz = mod(z + 8 - off, 8)
        b = 2 * zz + core
        dst = (kf.at[b], qs.at[zz], vf.at[b])[part]
        n = (off - 1) * 3 + part
        return remote(dst, dst, z_send.at[n], z_recv.at[n], z_dev(zz))

    def forward(off, part):
        ref = (kf, vf)[part].at[2 * mod(z + 8 - off, 8) + core]
        n = off * 2 + part
        return remote(ref, ref, f_send.at[n], f_recv.at[n], partner)

    def forward_arrival(off, part):
        ref = (kf, vf)[part].at[2 * mod(z + 8 - off, 8) + 1 - core]
        n = off * 2 + part
        return remote(ref, ref, f_send.at[n], f_recv.at[n], partner)

    for part in range(3):
        for off in z_order:
            z_copy(off, part).start()

    def columns(hc):
        return slice(FIRST[hc] * HS, (FIRST[hc] + HEADS_OF[hc]) * HS)

    def y_copy(hc, off):
        return remote(
            kvs[hc].at[off], pool[hc].at[pl.ds(2 * m, 2)],
            y_send.at[hc * 3 + off], y_recv.at[hc * 3 + off], y_dev(mod(m + 1 + off, 4)),
        )

    def y_arrival(hc, off):
        mm = mod(m + 3 - off, 4)
        return remote(
            kvs[hc].at[off], pool[hc].at[pl.ds(2 * mm, 2)],
            y_send.at[hc * 3 + off], y_recv.at[hc * 3 + off], y_dev(mm),
        )

    def y_local(hc):
        return pltpu.make_async_copy(kvs[hc].at[3], pool[hc].at[pl.ds(2 * m, 2)], y_loc.at[hc])

    def encode(hc):
        out = kvs[hc]

        def step(off, carry):
            t = mod(m + 1 + off, 4)
            tiles = [(n, j) for n in range(2) for j in range(HEADS_OF[hc])]
            cols = [
                pl.ds(pl.multiple_of((t * 8 + FIRST[hc] + j) * HS, HS), HS) for n, j in tiles
            ]
            q = [eqv[n, :, c] for (n, j), c in zip(tiles, cols)]
            k = [ekv[n, :, c] for (n, j), c in zip(tiles, cols)]
            v = [evv[n, :, c] for (n, j), c in zip(tiles, cols)]
            _, _, mixed = attend_all(q, k, v)
            for a, (n, j) in enumerate(tiles):
                at = slice(j * HS, (j + 1) * HS)
                out[off, n, 0, :, at] = (k[a].astype(F32) + mixed[a]).astype(BF16)
                out[off, n, 1, :, at] = (v[a].astype(F32) + mixed[a]).astype(BF16)

            @pl.when(off < 3)
            def _():
                y_copy(hc, off).start()

            @pl.when(off == 3)
            def _():
                y_local(hc).start()

            return carry

        lax.fori_loop(0, 4, step, 0)

    def q_copy(hc, off):
        mine = qb[hc].at[pl.ds(4 * g, 4)]
        return remote(
            mine, mine, q_send.at[hc * 3 + off], q_recv.at[hc * 3 + off], x_dev(mod(g + 1 + off, 4))
        )

    def q_arrival(hc, off):
        gg = mod(g + 3 - off, 4)
        theirs = qb[hc].at[pl.ds(4 * gg, 4)]
        return remote(
            theirs, theirs, q_send.at[hc * 3 + off], q_recv.at[hc * 3 + off], x_dev(gg)
        )

    def shift_queries():
        loads[0].wait()
        halo_copy.wait_recv()
        qf[0:ROWS, :] = cqv[...].astype(F32)
        qf[ROWS : ROWS + SPAN, :] = halo[...].astype(F32)
        for hc in range(CHUNKS):
            for u in range(4):
                first = SPAN - 1 + SPAN * u
                qb[hc][4 * g + u] = qf[first : first + SPAN, columns(hc)].astype(BF16)
            for off in range(3):
                q_copy(hc, off).start()

    def tables():
        for off in range(1, 4):
            gg = mod(g + 4 - off, 4)
            remote(
                idx_s, idx_all.at[gg], i_send.at[off - 1], i_recv.at[off - 1], x_dev(gg)
            ).wait_recv()
        idx_local.wait()
        to_smem = pltpu.make_async_copy(idx_all, idx_sm, misc.at[1])
        to_smem.start()
        to_smem.wait()

        def per_candidate(c, carry):
            ids = [idx_sm[c, 0, n] for n in range(8)]
            count = jnp.int32(0)
            rows = [c * 4] * CAP
            locals_ = [jnp.int32(0)] * CAP
            for n in range(8):
                mine = lax.shift_right_logical(ids[n], 7) == g
                for r in range(CAP):
                    hit = jnp.logical_and(mine, count == r)
                    rows[r] = jnp.where(hit, c * 4 + n // 2, rows[r])
                    locals_[r] = jnp.where(hit, ids[n] & 7, locals_[r])
                count = count + jnp.where(mine, 1, 0)
            for r in range(CAP):
                row_tab[c * 4 + r] = rows[r]
                id_tab[c * 4 + r] = locals_[r]
            return carry

        lax.fori_loop(0, 4, per_candidate, 0)
        targets = [lax.shift_right_logical(nbr[0, n % 2, n // 2], 7) for n in range(8)]
        for n in range(8):
            rank = jnp.int32(0)
            for e in range(n):
                rank = rank + jnp.where(targets[e] == targets[n], 1, 0)
            req_tab[n] = targets[n] * CAP + rank

    lane64 = lax.broadcasted_iota(jnp.int32, (SPAN, 128), 1)

    def o_copy(hc, off):
        return remote(
            os[hc].at[off], o_in[hc].at[pl.ds(4 * g, 4)],
            o_send.at[hc * 3 + off], o_recv.at[hc * 3 + off], x_dev(mod(g + 1 + off, 4)),
        )

    def t_copy(hc, off):
        return remote(
            ss[hc].at[off], st_in[hc].at[g],
            t_send.at[hc * 3 + off], t_recv.at[hc * 3 + off], x_dev(mod(g + 1 + off, 4)),
        )

    def o_local(hc):
        return (
            pltpu.make_async_copy(
                os[hc].at[3], o_in[hc].at[pl.ds(4 * g, 4)], o_loc.at[hc]
            ),
            pltpu.make_async_copy(ss[hc].at[3], st_in[hc].at[g], t_loc.at[hc]),
        )

    def cross(hc):
        for off in range(3):
            y_arrival(hc, off).wait_recv()
            q_arrival(hc, off).wait_recv()
        y_local(hc).wait()

        def step(off, carry):
            c = mod(g + 1 + off, 4)
            heads = range(HEADS_OF[hc])
            tiles = [(r, j) for r in range(CAP) for j in heads]
            q2 = [qb[hc][row_tab[c * 4 + r]] for r in range(CAP)]
            k2 = [pool[hc][id_tab[c * 4 + r], 0] for r in range(CAP)]
            v2 = [pool[hc][id_tab[c * 4 + r], 1] for r in range(CAP)]

            def split(x):
                return [x[r][:, j * HS : (j + 1) * HS] for r, j in tiles]

            tops, totals, mixed = attend_all(split(q2), split(k2), split(v2))
            logs = [top * SCALE + jnp.log2(total) for top, total in zip(tops, totals)]
            for a, (r, j) in enumerate(tiles):
                os[hc][off, r, :, j * HS : (j + 1) * HS] = mixed[a].astype(BF16)
            for r in range(CAP):
                row = jnp.where(lane64 == 0, logs[r * len(heads)], 0.0)
                for j in heads[1:]:
                    row = jnp.where(lane64 == j, logs[r * len(heads) + j], row)
                stage[r * SPAN : (r + 1) * SPAN, :] = row
            ss[hc][off] = jnp.transpose(stage[...])[0:8]

            @pl.when(off < 3)
            def _():
                o_copy(hc, off).start()
                t_copy(hc, off).start()

            @pl.when(off == 3)
            def _():
                for c_ in o_local(hc):
                    c_.start()

            return carry

        lax.fori_loop(0, 4, step, 0)

    def b_copy(i, k):
        return remote(
            os_self.at[i], self_out.at[0, :, own], b_send.at[k], b_recv.at[k], z_dev(i)
        )

    KEYS = 512
    key_iota = lax.broadcasted_iota(jnp.int32, (ROWS, KEYS), 1)
    row_iota = lax.broadcasted_iota(jnp.int32, (ROWS, KEYS), 0)

    def self_attend():
        for n, i in enumerate(reversed(range(8))):
            q = qs[i]
            top = None
            for j in range(i + 1):
                sc = scores_of(q, kf[2 * j : 2 * j + 2].reshape(KEYS, HS))
                if j == i:
                    sc = jnp.where(key_iota <= row_iota + core * ROWS, sc, MASKED)
                sc_buf[j] = sc
                high = fold(sc, jnp.maximum)
                top = high if top is None else jnp.maximum(top, high)
            top = jnp.max(top, axis=1, keepdims=True) * SCALE
            if n == 0:
                for off in range(8):
                    forward_arrival(off, 1).wait_recv()
            total = acc = None
            for j in range(i + 1):
                w = jnp.exp2(sc_buf[j] * SCALE - top)
                low = fold(w, jnp.add)
                part = mix(w, vf[2 * j : 2 * j + 2].reshape(KEYS, HS))
                total, acc = (low, part) if total is None else (total + low, acc + part)
            total = jnp.sum(total, axis=1, keepdims=True)
            pos = (2 * i + core) * ROWS + lax.broadcasted_iota(jnp.int32, (ROWS, HS), 0)
            os_self[i] = jnp.where(pos < seq_len, acc * (1.0 / total), 0.0).astype(BF16)
        for k in (3, 2, 4, 1, 5, 0, 6):
            b_copy(mod(z + 1 + k, 8), k).start()
        pltpu.make_async_copy(os_self.at[z], self_out.at[0, :, own], misc.at[10]).start()

    first_pos = s * ROWS

    def o_arrivals(hc):
        for off in range(3):
            gg = mod(g + 3 - off, 4)
            n = hc * 3 + off
            remote(
                os[hc].at[off], o_in[hc].at[pl.ds(4 * gg, 4)], o_send.at[n], o_recv.at[n], x_dev(gg)
            ).wait_recv()
            remote(
                ss[hc].at[off], st_in[hc].at[gg], t_send.at[n], t_recv.at[n], x_dev(gg)
            ).wait_recv()
        for c in o_local(hc):
            c.wait()

    def tail_copy(hc):
        return remote(tail_s[hc], tail_in[hc], e_send.at[hc], e_recv.at[hc], ahead)

    def out_copy(hc):
        return pltpu.make_async_copy(
            co.at[:, columns(hc)], cross_out.at[0, :, columns(hc)], c_sem.at[hc]
        )

    def live(first, rows, width):
        pos = first_pos + first + lax.broadcasted_iota(jnp.int32, (rows, width), 0)
        return jnp.logical_and(pos >= SPAN - 1, pos < seq_len)

    def combine(hc):
        width = HEADS_OF[hc] * HS
        cols = columns(hc)
        o_arrivals(hc)
        logs = jnp.concatenate([st_in[hc][...].reshape(32, 256), jnp.zeros((96, 256), F32)], axis=0)
        turned = jnp.transpose(logs)
        for gg in range(4):
            part = turned if gg == 0 else pltpu.roll(turned, 128 - 8 * gg, 1)
            for r in range(CAP):
                stat[gg * CAP + r] = part[r * SPAN : (r + 1) * SPAN, :]
        of[ROWS + 56 : ROWS + 64, cols] = jnp.zeros((8, width), F32)
        for u in (3, 0, 1, 2):
            s0, s1 = req_tab[2 * u], req_tab[2 * u + 1]
            l0, l1 = stat[s0], stat[s1]
            top = jnp.maximum(l0, l1)
            w0, w1 = jnp.exp2(l0 - top), jnp.exp2(l1 - top)
            inv = 1.0 / (w0 + w1)
            w0, w1 = w0 * inv, w1 * inv
            o0, o1 = o_in[hc][s0], o_in[hc][s1]
            first = SPAN - 1 + SPAN * u
            for j in range(HEADS_OF[hc]):
                at = slice(j * HS, (j + 1) * HS)
                of[first : first + SPAN, cols.start + j * HS : cols.start + (j + 1) * HS] = (
                    o0[:, at].astype(F32) * w0[:, j : j + 1]
                    + o1[:, at].astype(F32) * w1[:, j : j + 1]
                )
            if u == 3:
                tail_s[hc][...] = of[ROWS : ROWS + SPAN, cols].astype(BF16)
                tail_copy(hc).start()
        co[SPAN:ROWS, cols] = jnp.where(
            live(SPAN, ROWS - SPAN, width), of[SPAN:ROWS, cols], 0.0
        ).astype(BF16)

    def finish(hc):
        width = HEADS_OF[hc] * HS
        cols = columns(hc)
        tail_copy(hc).wait_recv()
        row = lax.broadcasted_iota(jnp.int32, (SPAN, width), 0)
        head = jnp.where(row < SPAN - 1, tail_in[hc][...].astype(F32), of[0:SPAN, cols])
        co[0:SPAN, cols] = jnp.where(live(0, SPAN, width), head, 0.0).astype(BF16)
        out_copy(hc).start()

    for c in loads[1:]:
        c.wait()
    encode(0)
    shift_queries()
    for hc in range(1, CHUNKS):
        encode(hc)
    for c in local_in:
        c.wait()
    for part in range(2):
        forward(0, part).start()
    tables()
    cross(0)
    for off in z_order:
        z_arrival(off, 0).wait_recv()
        forward(off, 0).start()
    cross(1)
    for off in z_order:
        z_arrival(off, 1).wait_recv()
    cross(2)
    for off in z_order:
        z_arrival(off, 2).wait_recv()
        forward(off, 1).start()
    for off in range(8):
        forward_arrival(off, 0).wait_recv()
    self_attend()
    cross(3)
    combine(0)
    combine(1)
    cross(4)
    combine(2)
    combine(3)
    for hc in range(3):
        finish(hc)
    combine(4)
    finish(3)
    finish(4)

    pltpu.make_async_copy(os_self.at[z], self_out.at[0, :, own], misc.at[10]).wait()
    for k in range(7):
        src = mod(z + 7 - k, 8)
        cols = pl.ds(pl.multiple_of(src * HS, HS), HS)
        remote(
            os_self.at[z], self_out.at[0, :, cols], b_send.at[k], b_recv.at[k], z_dev(src)
        ).wait_recv()
        b_copy(mod(z + 1 + k, 8), k).wait_send()
    halo_copy.wait_send()
    for c in idx_copies:
        c.wait_send()
    for part in range(3):
        for off in z_order:
            z_copy(off, part).wait_send()
    for off in range(8):
        for part in range(2):
            forward(off, part).wait_send()
    for hc in range(CHUNKS):
        for off in range(3):
            y_copy(hc, off).wait_send()
            q_copy(hc, off).wait_send()
            o_copy(hc, off).wait_send()
            t_copy(hc, off).wait_send()
        tail_copy(hc).wait_send()
        out_copy(hc).wait()


def local(*args):
    dec_query, dec_key, dec_value, cross_query, enc_query, enc_key, enc_value, nbr_index, seq_lengths = args
    any_ = pl.BlockSpec(memory_space=pl.ANY)
    smem = pl.BlockSpec(memory_space=pltpu.SMEM)
    V = pltpu.VMEM
    dma = lambda n: pltpu.SemaphoreType.DMA((n,))
    scratch = [V((2, 128, 4096), BF16)] * 3
    scratch += [V((ROWS, WIDTH), BF16), V((SPAN, WIDTH), BF16), V((ROWS + SPAN, WIDTH), F32)]
    scratch += [
        V((256, 128), F32), V((16, SPAN, 128), F32), V((ROWS + SPAN, WIDTH), F32),
        V((ROWS, WIDTH), BF16),
    ]
    scratch += [
        V((8, ROWS, HS), BF16), V((16, ROWS, HS), BF16), V((16, ROWS, HS), BF16),
        V((8, ROWS, HS), BF16), V((8, ROWS, 512), F32),
    ]
    scratch += [
        V((8, 128), jnp.int32), V((4, 8, 128), jnp.int32), pltpu.SMEM((4, 8, 128), jnp.int32),
        pltpu.SMEM((16,), jnp.int32), pltpu.SMEM((16,), jnp.int32), pltpu.SMEM((8,), jnp.int32),
    ]
    per = 3 * CHUNKS
    scratch += [
        dma(n)
        for n in (
            7, 21, 21, 16, 16, per, per, CHUNKS, per, per, per, per, per, per, CHUNKS, CHUNKS,
            3, 3, 7, 7, 1, 1, CHUNKS, CHUNKS, CHUNKS, 12,
        )
    ]
    widths = [n * HS for n in HEADS_OF]
    for form in (
        lambda w: V((4, 2, 2, 128, w), BF16),
        lambda w: V((8, 2, 128, w), BF16),
        lambda w: V((16, SPAN, w), BF16),
        lambda w: V((4, 4, SPAN, w), BF16),
        lambda w: V((4, 8, 256), F32),
        lambda w: V((16, SPAN, w), BF16),
        lambda w: V((4, 8, 256), F32),
        lambda w: V((SPAN, w), BF16),
        lambda w: V((SPAN, w), BF16),
    ):
        scratch += [form(w) for w in widths]
    shape = jax.ShapeDtypeStruct((1, ROWS, WIDTH), BF16)
    return pl.pallas_call(
        kernel,
        out_shape=(shape, shape),
        in_specs=[smem, smem] + [any_] * 7,
        out_specs=(any_, any_),
        scratch_shapes=scratch,
        compiler_params=pltpu.CompilerParams(
            collective_id=0, has_side_effects=True, vmem_limit_bytes=56 << 20
        ),
        name="retro_block",
    )(jnp.transpose(nbr_index, (0, 2, 1)), seq_lengths, dec_query, dec_key, dec_value, cross_query, enc_query, enc_key, enc_value)


def solution(mesh):
    rows = P("grp", "seq", "mp")
    store = P(("grp", "seq", "mp"), None, None)
    return jax.shard_map(
        local,
        mesh=mesh,
        in_specs=(rows, rows, rows, rows, store, store, store, P("grp", "seq", None), P("grp")),
        out_specs=(rows, rows),
        check_vma=False,
    )
```

```python
import functools
import math

import jax
import jax.numpy as jnp
from jax import lax
from jax.experimental import pallas as pl
from jax.experimental.pallas import tpu as pltpu
from jax.sharding import PartitionSpec as P

HS = 128
SPAN = 64
CAP = 4
HEADS_OF = (1, 2, 2, 2, 1)
FIRST = (0, 1, 3, 5, 7)
CHUNKS = len(HEADS_OF)
ROWS = 256
WIDTH = 1024
SCALE = HS ** (-0.5) * math.log2(math.e)
MASKED = -1e30
MESH = pl.DeviceIdType.MESH
F32 = jnp.float32
BF16 = jnp.bfloat16
NT = (((1,), (1,)), ((), ()))


def mod(a, n):
    return lax.rem(a, n)


def scores_of(q, k):
    return lax.dot_general(q, k, NT, preferred_element_type=F32)


def mix(weights, v):
    return jnp.dot(weights.astype(BF16), v, preferred_element_type=F32)


def fold(x, op):
    parts = [x[:, a : a + HS] for a in range(0, x.shape[1], HS)]
    while len(parts) > 1:
        parts = [op(parts[a], parts[a + 1]) for a in range(0, len(parts), 2)]
    return parts[0]


def attend_all(queries, keys, values):
    scores = [scores_of(q, k) for q, k in zip(queries, keys)]
    tops = [jnp.max(x, axis=1, keepdims=True) for x in scores]
    weights = [jnp.exp2((x - top) * SCALE) for x, top in zip(scores, tops)]
    totals = [jnp.sum(w, axis=1, keepdims=True) for w in weights]
    sums = [mix(w, v) for w, v in zip(weights, values)]
    return tops, totals, [x * (1.0 / total) for x, total in zip(sums, totals)]


def kernel(
    nbr, lens, dq, dk, dv, cq, eq, ek, ev,
    self_out, cross_out,
    eqv, ekv, evv, cqv, halo, qf,
    stage, stat, of, co,
    qs, kf, vf, os_self, sc_buf, p_buf, tot_buf,
    idx_s, idx_all, idx_sm, row_tab, id_tab, req_tab,
    load_sem, z_send, z_recv, f_send, f_recv, y_send, y_recv, y_loc,
    q_send, q_recv, o_send, o_recv, t_send, t_recv, o_loc, t_loc, i_send, i_recv,
    b_send, b_recv, h_send, h_recv, e_send, e_recv, c_sem, misc,
    *chunked,
):
    kvs, pool, qb, os, ss, o_in, st_in, tail_s, tail_in = (
        chunked[n * CHUNKS : (n + 1) * CHUNKS] for n in range(9)
    )
    g = lax.axis_index("grp")
    s = lax.axis_index("seq")
    m = lax.axis_index("mp")
    z = lax.div(s, 2)
    core = lax.rem(s, 2)
    seq_len = lens[0]

    def z_dev(zz):
        return (g, 2 * zz + core, m)

    def y_dev(mm):
        return (g, s, mm)

    def x_dev(gg):
        return (gg, s, m)

    partner = (g, s + 1 - 2 * core, m)
    other = (g, mod(s + 15 + 2 * core, 16), m)
    behind = (g, mod(s + 15, 16), m)
    ahead = (g, mod(s + 1, 16), m)

    def remote(src, dst, send, recv, dev):
        return pltpu.make_async_remote_copy(
            src_ref=src, dst_ref=dst, send_sem=send, recv_sem=recv,
            device_id=dev, device_id_type=MESH,
        )

    loads = [
        pltpu.make_async_copy(src, dst, load_sem.at[n])
        for n, (src, dst) in enumerate(((cq.at[0], cqv), (eq, eqv), (ek, ekv), (ev, evv)))
    ]
    for c in loads:
        c.start()
    own = pl.ds(pl.multiple_of(z * HS, HS), HS)
    local_in = [
        pltpu.make_async_copy(dq.at[0, :, own], qs.at[z], load_sem.at[4]),
        pltpu.make_async_copy(dk.at[0, :, own], kf.at[s], load_sem.at[5]),
        pltpu.make_async_copy(dv.at[0, :, own], vf.at[s], load_sem.at[6]),
    ]
    for c in local_in:
        c.start()

    bar = pltpu.get_barrier_semaphore()
    peers = [z_dev(mod(z + off, 8)) for off in range(1, 8)]
    peers += [y_dev(mod(m + off, 4)) for off in range(1, 4)]
    peers += [x_dev(mod(g + off, 4)) for off in range(1, 4)]
    peers += [partner, other]
    for dev in peers:
        pl.semaphore_signal(bar, inc=1, device_id=dev, device_id_type=MESH)
    pl.semaphore_wait(bar, len(peers))

    halo_copy = remote(cq.at[0, pl.ds(0, SPAN)], halo, h_send.at[0], h_recv.at[0], behind)
    halo_copy.start()

    lane8 = lax.broadcasted_iota(jnp.int32, (8, 128), 1)
    packed = jnp.zeros((8, 128), jnp.int32)
    for n in range(8):
        packed = jnp.where(lane8 == n, nbr[0, n % 2, n // 2], packed)
    idx_s[...] = packed
    idx_copies = [
        remote(idx_s, idx_all.at[g], i_send.at[off - 1], i_recv.at[off - 1], x_dev(mod(g + off, 4)))
        for off in range(1, 4)
    ]
    for c in idx_copies:
        c.start()
    idx_local = pltpu.make_async_copy(idx_s, idx_all.at[g], misc.at[0])
    idx_local.start()

    z_order = (4, 3, 5, 2, 6, 1, 7)

    def z_copy(off, part):
        zz = mod(z + off, 8)
        cols = pl.ds(pl.multiple_of(zz * HS, HS), HS)
        src = (dk, dq, dv)[part].at[0, :, cols]
        dst = (kf.at[s], qs.at[z], vf.at[s])[part]
        n = (off - 1) * 3 + part
        return remote(src, dst, z_send.at[n], z_recv.at[n], z_dev(zz))

    def z_arrival(off, part):
        zz = mod(z + 8 - off, 8)
        b = 2 * zz + core
        dst = (kf.at[b], qs.at[zz], vf.at[b])[part]
        n = (off - 1) * 3 + part
        return remote(dst, dst, z_send.at[n], z_recv.at[n], z_dev(zz))

    def forward(off, part):
        ref = (kf, vf)[part].at[2 * mod(z + 8 - off, 8) + core]
        n = off * 2 + part
        return remote(ref, ref, f_send.at[n], f_recv.at[n], partner)

    def forward_arrival(off, part):
        ref = (kf, vf)[part].at[2 * mod(z + 8 - off, 8) + 1 - core]
        n = off * 2 + part
        return remote(ref, ref, f_send.at[n], f_recv.at[n], partner)

    for part in range(3):
        for off in z_order:
            z_copy(off, part).start()

    def columns(hc):
        return slice(FIRST[hc] * HS, (FIRST[hc] + HEADS_OF[hc]) * HS)

    def y_copy(hc, off):
        return remote(
            kvs[hc].at[off], pool[hc].at[pl.ds(2 * m, 2)],
            y_send.at[hc * 3 + off], y_recv.at[hc * 3 + off], y_dev(mod(m + 1 + off, 4)),
        )

    def y_arrival(hc, off):
        mm = mod(m + 3 - off, 4)
        return remote(
            kvs[hc].at[off], pool[hc].at[pl.ds(2 * mm, 2)],
            y_send.at[hc * 3 + off], y_recv.at[hc * 3 + off], y_dev(mm),
        )

    def y_local(hc):
        return pltpu.make_async_copy(kvs[hc].at[3], pool[hc].at[pl.ds(2 * m, 2)], y_loc.at[hc])

    def encode(hc):
        out = kvs[hc]

        def step(off, carry):
            t = mod(m + 1 + off, 4)
            tiles = [(n, j) for n in range(2) for j in range(HEADS_OF[hc])]
            cols = [
                pl.ds(pl.multiple_of((t * 8 + FIRST[hc] + j) * HS, HS), HS) for n, j in tiles
            ]
            q = [eqv[n, :, c] for (n, j), c in zip(tiles, cols)]
            k = [ekv[n, :, c] for (n, j), c in zip(tiles, cols)]
            v = [evv[n, :, c] for (n, j), c in zip(tiles, cols)]
            _, _, mixed = attend_all(q, k, v)
            for a, (n, j) in enumerate(tiles):
                at = slice(j * HS, (j + 1) * HS)
                out[off, n, 0, :, at] = (k[a].astype(F32) + mixed[a]).astype(BF16)
                out[off, n, 1, :, at] = (v[a].astype(F32) + mixed[a]).astype(BF16)

            @pl.when(off < 3)
            def _():
                y_copy(hc, off).start()

            @pl.when(off == 3)
            def _():
                y_local(hc).start()

            return carry

        lax.fori_loop(0, 4, step, 0)

    def q_copy(hc, off):
        mine = qb[hc].at[pl.ds(4 * g, 4)]
        return remote(
            mine, mine, q_send.at[hc * 3 + off], q_recv.at[hc * 3 + off], x_dev(mod(g + 1 + off, 4))
        )

    def q_arrival(hc, off):
        gg = mod(g + 3 - off, 4)
        theirs = qb[hc].at[pl.ds(4 * gg, 4)]
        return remote(
            theirs, theirs, q_send.at[hc * 3 + off], q_recv.at[hc * 3 + off], x_dev(gg)
        )

    def shift_queries():
        loads[0].wait()
        halo_copy.wait_recv()
        qf[0:ROWS, :] = cqv[...].astype(F32)
        qf[ROWS : ROWS + SPAN, :] = halo[...].astype(F32)
        for hc in range(CHUNKS):
            for u in range(4):
                first = SPAN - 1 + SPAN * u
                qb[hc][4 * g + u] = qf[first : first + SPAN, columns(hc)].astype(BF16)
            for off in range(3):
                q_copy(hc, off).start()

    def tables():
        for off in range(1, 4):
            gg = mod(g + 4 - off, 4)
            remote(
                idx_s, idx_all.at[gg], i_send.at[off - 1], i_recv.at[off - 1], x_dev(gg)
            ).wait_recv()
        idx_local.wait()
        to_smem = pltpu.make_async_copy(idx_all, idx_sm, misc.at[1])
        to_smem.start()
        to_smem.wait()

        def per_candidate(c, carry):
            ids = [idx_sm[c, 0, n] for n in range(8)]
            count = jnp.int32(0)
            rows = [c * 4] * CAP
            locals_ = [jnp.int32(0)] * CAP
            for n in range(8):
                mine = lax.shift_right_logical(ids[n], 7) == g
                for r in range(CAP):
                    hit = jnp.logical_and(mine, count == r)
                    rows[r] = jnp.where(hit, c * 4 + n // 2, rows[r])
                    locals_[r] = jnp.where(hit, ids[n] & 7, locals_[r])
                count = count + jnp.where(mine, 1, 0)
            for r in range(CAP):
                row_tab[c * 4 + r] = rows[r]
                id_tab[c * 4 + r] = locals_[r]
            return carry

        lax.fori_loop(0, 4, per_candidate, 0)
        targets = [lax.shift_right_logical(nbr[0, n % 2, n // 2], 7) for n in range(8)]
        for n in range(8):
            rank = jnp.int32(0)
            for e in range(n):
                rank = rank + jnp.where(targets[e] == targets[n], 1, 0)
            req_tab[n] = targets[n] * CAP + rank

    lane64 = lax.broadcasted_iota(jnp.int32, (SPAN, 128), 1)

    def o_copy(hc, off):
        return remote(
            os[hc].at[off], o_in[hc].at[pl.ds(4 * g, 4)],
            o_send.at[hc * 3 + off], o_recv.at[hc * 3 + off], x_dev(mod(g + 1 + off, 4)),
        )

    def t_copy(hc, off):
        return remote(
            ss[hc].at[off], st_in[hc].at[g],
            t_send.at[hc * 3 + off], t_recv.at[hc * 3 + off], x_dev(mod(g + 1 + off, 4)),
        )

    def o_local(hc):
        return (
            pltpu.make_async_copy(
                os[hc].at[3], o_in[hc].at[pl.ds(4 * g, 4)], o_loc.at[hc]
            ),
            pltpu.make_async_copy(ss[hc].at[3], st_in[hc].at[g], t_loc.at[hc]),
        )

    def cross(hc):
        for off in range(3):
            y_arrival(hc, off).wait_recv()
            q_arrival(hc, off).wait_recv()
        y_local(hc).wait()

        def step(off, carry):
            c = mod(g + 1 + off, 4)
            heads = range(HEADS_OF[hc])
            tiles = [(r, j) for r in range(CAP) for j in heads]
            q2 = [qb[hc][row_tab[c * 4 + r]] for r in range(CAP)]
            k2 = [pool[hc][id_tab[c * 4 + r], 0] for r in range(CAP)]
            v2 = [pool[hc][id_tab[c * 4 + r], 1] for r in range(CAP)]

            def split(x):
                return [x[r][:, j * HS : (j + 1) * HS] for r, j in tiles]

            tops, totals, mixed = attend_all(split(q2), split(k2), split(v2))
            logs = [top * SCALE + jnp.log2(total) for top, total in zip(tops, totals)]
            for a, (r, j) in enumerate(tiles):
                os[hc][off, r, :, j * HS : (j + 1) * HS] = mixed[a].astype(BF16)
            for r in range(CAP):
                row = jnp.where(lane64 == 0, logs[r * len(heads)], 0.0)
                for j in heads[1:]:
                    row = jnp.where(lane64 == j, logs[r * len(heads) + j], row)
                stage[r * SPAN : (r + 1) * SPAN, :] = row
            ss[hc][off] = jnp.transpose(stage[...])[0:8]

            @pl.when(off < 3)
            def _():
                o_copy(hc, off).start()
                t_copy(hc, off).start()

            @pl.when(off == 3)
            def _():
                for c_ in o_local(hc):
                    c_.start()

            return carry

        lax.fori_loop(0, 4, step, 0)

    def b_copy(i, k):
        return remote(
            os_self.at[i], self_out.at[0, :, own], b_send.at[k], b_recv.at[k], z_dev(i)
        )

    KEYS = 512
    key_iota = lax.broadcasted_iota(jnp.int32, (ROWS, KEYS), 1)
    row_iota = lax.broadcasted_iota(jnp.int32, (ROWS, KEYS), 0)

    def self_weights():
        for i in reversed(range(8)):
            q = qs[i]
            top = None
            for j in range(i + 1):
                sc = scores_of(q, kf[2 * j : 2 * j + 2].reshape(KEYS, HS))
                if j == i:
                    sc = jnp.where(key_iota <= row_iota + core * ROWS, sc, MASKED)
                sc_buf[j] = sc
                high = fold(sc, jnp.maximum)
                top = high if top is None else jnp.maximum(top, high)
            top = jnp.max(top, axis=1, keepdims=True) * SCALE
            total = None
            for j in range(i + 1):
                w = jnp.exp2(sc_buf[j] * SCALE - top)
                p_buf[i, :, j * KEYS : (j + 1) * KEYS] = w.astype(BF16)
                low = fold(w, jnp.add)
                total = low if total is None else total + low
            tot_buf[i] = total

    def self_values():
        for i in reversed(range(8)):
            acc = jnp.dot(
                p_buf[i, :, 0 : (i + 1) * KEYS],
                vf[0 : 2 * i + 2].reshape((i + 1) * KEYS, HS),
                preferred_element_type=F32,
            )
            total = jnp.sum(tot_buf[i], axis=1, keepdims=True)
            pos = (2 * i + core) * ROWS + lax.broadcasted_iota(jnp.int32, (ROWS, HS), 0)
            os_self[i] = jnp.where(pos < seq_len, acc * (1.0 / total), 0.0).astype(BF16)
        for k in (3, 2, 4, 1, 5, 0, 6):
            b_copy(mod(z + 1 + k, 8), k).start()
        pltpu.make_async_copy(os_self.at[z], self_out.at[0, :, own], misc.at[10]).start()

    first_pos = s * ROWS

    def o_arrivals(hc):
        for off in range(3):
            gg = mod(g + 3 - off, 4)
            n = hc * 3 + off
            remote(
                os[hc].at[off], o_in[hc].at[pl.ds(4 * gg, 4)], o_send.at[n], o_recv.at[n], x_dev(gg)
            ).wait_recv()
            remote(
                ss[hc].at[off], st_in[hc].at[gg], t_send.at[n], t_recv.at[n], x_dev(gg)
            ).wait_recv()
        for c in o_local(hc):
            c.wait()

    def tail_copy(hc):
        return remote(tail_s[hc], tail_in[hc], e_send.at[hc], e_recv.at[hc], ahead)

    def out_copy(hc):
        return pltpu.make_async_copy(
            co.at[:, columns(hc)], cross_out.at[0, :, columns(hc)], c_sem.at[hc]
        )

    def live(first, rows, width):
        pos = first_pos + first + lax.broadcasted_iota(jnp.int32, (rows, width), 0)
        return jnp.logical_and(pos >= SPAN - 1, pos < seq_len)

    def combine(hc):
        width = HEADS_OF[hc] * HS
        cols = columns(hc)
        o_arrivals(hc)
        logs = jnp.concatenate([st_in[hc][...].reshape(32, 256), jnp.zeros((96, 256), F32)], axis=0)
        turned = jnp.transpose(logs)
        for gg in range(4):
            part = turned if gg == 0 else pltpu.roll(turned, 128 - 8 * gg, 1)
            for r in range(CAP):
                stat[gg * CAP + r] = part[r * SPAN : (r + 1) * SPAN, :]
        of[ROWS + 56 : ROWS + 64, cols] = jnp.zeros((8, width), F32)
        for u in (3, 0, 1, 2):
            s0, s1 = req_tab[2 * u], req_tab[2 * u + 1]
            l0, l1 = stat[s0], stat[s1]
            top = jnp.maximum(l0, l1)
            w0, w1 = jnp.exp2(l0 - top), jnp.exp2(l1 - top)
            inv = 1.0 / (w0 + w1)
            w0, w1 = w0 * inv, w1 * inv
            o0, o1 = o_in[hc][s0], o_in[hc][s1]
            first = SPAN - 1 + SPAN * u
            for j in range(HEADS_OF[hc]):
                at = slice(j * HS, (j + 1) * HS)
                of[first : first + SPAN, cols.start + j * HS : cols.start + (j + 1) * HS] = (
                    o0[:, at].astype(F32) * w0[:, j : j + 1]
                    + o1[:, at].astype(F32) * w1[:, j : j + 1]
                )
            if u == 3:
                tail_s[hc][...] = of[ROWS : ROWS + SPAN, cols].astype(BF16)
                tail_copy(hc).start()
        co[SPAN:ROWS, cols] = jnp.where(
            live(SPAN, ROWS - SPAN, width), of[SPAN:ROWS, cols], 0.0
        ).astype(BF16)

    def finish(hc):
        width = HEADS_OF[hc] * HS
        cols = columns(hc)
        tail_copy(hc).wait_recv()
        row = lax.broadcasted_iota(jnp.int32, (SPAN, width), 0)
        head = jnp.where(row < SPAN - 1, tail_in[hc][...].astype(F32), of[0:SPAN, cols])
        co[0:SPAN, cols] = jnp.where(live(0, SPAN, width), head, 0.0).astype(BF16)
        out_copy(hc).start()

    def sent(hc):
        for off in range(3):
            y_copy(hc, off).wait_send()
            q_copy(hc, off).wait_send()

    def answered(hc):
        for off in range(3):
            o_copy(hc, off).wait_send()
            t_copy(hc, off).wait_send()
        tail_copy(hc).wait_send()

    for c in loads[1:]:
        c.wait()
    encode(0)
    shift_queries()
    for hc in range(1, CHUNKS):
        encode(hc)
    for c in local_in:
        c.wait()
    for part in range(2):
        forward(0, part).start()
    tables()
    cross(0)
    for off in z_order:
        z_arrival(off, 0).wait_recv()
        forward(off, 0).start()
    halo_copy.wait_send()
    for c in idx_copies:
        c.wait_send()
    cross(1)
    sent(0)
    for off in z_order:
        z_arrival(off, 1).wait_recv()
    for off in range(8):
        forward_arrival(off, 0).wait_recv()
    self_weights()
    cross(2)
    for off in z_order:
        z_arrival(off, 2).wait_recv()
        forward(off, 1).start()
    sent(1)
    for off in z_order:
        for part in range(3):
            z_copy(off, part).wait_send()
    for off in range(8):
        forward_arrival(off, 1).wait_recv()
    self_values()
    combine(0)
    cross(3)
    combine(1)
    cross(4)
    sent(2)
    sent(3)
    sent(4)
    for off in range(8):
        for part in range(2):
            forward(off, part).wait_send()
    combine(2)
    finish(0)
    finish(1)
    combine(3)
    answered(0)
    answered(1)
    finish(2)
    combine(4)
    finish(3)
    answered(2)
    answered(3)
    finish(4)
    answered(4)

    pltpu.make_async_copy(os_self.at[z], self_out.at[0, :, own], misc.at[10]).wait()
    for k in range(7):
        src = mod(z + 7 - k, 8)
        cols = pl.ds(pl.multiple_of(src * HS, HS), HS)
        remote(
            os_self.at[z], self_out.at[0, :, cols], b_send.at[k], b_recv.at[k], z_dev(src)
        ).wait_recv()
        b_copy(mod(z + 1 + k, 8), k).wait_send()
    for hc in range(CHUNKS):
        out_copy(hc).wait()


def place(a_ref, b_ref, a_out, b_out, held, in_sem, out_sem):
    pieces = [
        (src.at[0, pl.ds(half * 128, 128)], dst.at[0, pl.ds(half * 128, 128)])
        for half in range(2)
        for src, dst in ((a_ref, a_out), (b_ref, b_out))
    ]
    loads = [
        pltpu.make_async_copy(src, held.at[n], in_sem.at[n]) for n, (src, _) in enumerate(pieces)
    ]
    stores = [
        pltpu.make_async_copy(held.at[n], dst, out_sem.at[n]) for n, (_, dst) in enumerate(pieces)
    ]
    for c in loads:
        c.start()
    for load, store in zip(loads, stores):
        load.wait()
        store.start()
    for c in stores:
        c.wait()


def local(*args):
    dec_query, dec_key, dec_value, cross_query, enc_query, enc_key, enc_value, nbr_index, seq_lengths = args
    any_ = pl.BlockSpec(memory_space=pl.ANY)
    smem = pl.BlockSpec(memory_space=pltpu.SMEM)
    V = pltpu.VMEM
    dma = lambda n: pltpu.SemaphoreType.DMA((n,))
    scratch = [V((2, 128, 4096), BF16)] * 3
    scratch += [V((ROWS, WIDTH), BF16), V((SPAN, WIDTH), BF16), V((ROWS + SPAN, WIDTH), F32)]
    scratch += [
        V((256, 128), F32), V((16, SPAN, 128), F32), V((ROWS + SPAN, WIDTH), F32),
        V((ROWS, WIDTH), BF16),
    ]
    scratch += [
        V((8, ROWS, HS), BF16), V((16, ROWS, HS), BF16), V((16, ROWS, HS), BF16),
        V((8, ROWS, HS), BF16), V((8, ROWS, 512), F32), V((8, ROWS, 4096), BF16), V((8, ROWS, HS), F32),
    ]
    scratch += [
        V((8, 128), jnp.int32), V((4, 8, 128), jnp.int32), pltpu.SMEM((4, 8, 128), jnp.int32),
        pltpu.SMEM((16,), jnp.int32), pltpu.SMEM((16,), jnp.int32), pltpu.SMEM((8,), jnp.int32),
    ]
    per = 3 * CHUNKS
    scratch += [
        dma(n)
        for n in (
            7, 21, 21, 16, 16, per, per, CHUNKS, per, per, per, per, per, per, CHUNKS, CHUNKS,
            3, 3, 7, 7, 1, 1, CHUNKS, CHUNKS, CHUNKS, 12,
        )
    ]
    widths = [n * HS for n in HEADS_OF]
    for form in (
        lambda w: V((4, 2, 2, 128, w), BF16),
        lambda w: V((8, 2, 128, w), BF16),
        lambda w: V((16, SPAN, w), BF16),
        lambda w: V((4, 4, SPAN, w), BF16),
        lambda w: V((4, 8, 256), F32),
        lambda w: V((16, SPAN, w), BF16),
        lambda w: V((4, 8, 256), F32),
        lambda w: V((SPAN, w), BF16),
        lambda w: V((SPAN, w), BF16),
    ):
        scratch += [form(w) for w in widths]
    shape = jax.ShapeDtypeStruct((1, ROWS, WIDTH), BF16)
    both = pl.pallas_call(
        kernel,
        out_shape=(shape, shape),
        in_specs=[smem, smem] + [any_] * 7,
        out_specs=(any_, any_),
        scratch_shapes=scratch,
        compiler_params=pltpu.CompilerParams(
            collective_id=0, has_side_effects=True, vmem_limit_bytes=56 << 20
        ),
        name="retro_block",
    )(jnp.transpose(nbr_index, (0, 2, 1)), seq_lengths, dec_query, dec_key, dec_value, cross_query, enc_query, enc_key, enc_value)
    return pl.pallas_call(
        place,
        out_shape=(shape, shape),
        in_specs=[any_] * 2,
        out_specs=(any_, any_),
        scratch_shapes=[V((4, 128, WIDTH), BF16), dma(4), dma(4)],
        name="place",
    )(*both)


def solution(mesh):
    rows = P("grp", "seq", "mp")
    store = P(("grp", "seq", "mp"), None, None)
    return jax.shard_map(
        local,
        mesh=mesh,
        in_specs=(rows, rows, rows, rows, store, store, store, P("grp", "seq", None), P("grp")),
        out_specs=(rows, rows),
        check_vma=False,
    )
```

```python
import functools
import math

import jax
import jax.numpy as jnp
from jax import lax
from jax.experimental import pallas as pl
from jax.experimental.pallas import tpu as pltpu
from jax.sharding import PartitionSpec as P

HS = 128
SPAN = 64
CAP = 4
HEADS_OF = (1, 2, 2, 2, 1)
FIRST = (0, 1, 3, 5, 7)
CHUNKS = len(HEADS_OF)
ROWS = 256
WIDTH = 1024
SCALE = HS ** (-0.5) * math.log2(math.e)
MASKED = -1e30
MESH = pl.DeviceIdType.MESH
F32 = jnp.float32
BF16 = jnp.bfloat16
NT = (((1,), (1,)), ((), ()))


def mod(a, n):
    return lax.rem(a, n)


def scores_of(q, k):
    return lax.dot_general(q, k, NT, preferred_element_type=F32)


def mix(weights, v):
    return jnp.dot(weights.astype(BF16), v, preferred_element_type=F32)


def fold(x, op):
    parts = [x[:, a : a + HS] for a in range(0, x.shape[1], HS)]
    while len(parts) > 1:
        parts = [op(parts[a], parts[a + 1]) for a in range(0, len(parts), 2)]
    return parts[0]


def attend_all(queries, keys, values):
    scores = [scores_of(q, k) for q, k in zip(queries, keys)]
    tops = [jnp.max(x, axis=1, keepdims=True) for x in scores]
    weights = [jnp.exp2((x - top) * SCALE) for x, top in zip(scores, tops)]
    totals = [jnp.sum(w, axis=1, keepdims=True) for w in weights]
    sums = [mix(w, v) for w, v in zip(weights, values)]
    return tops, totals, [x * (1.0 / total) for x, total in zip(sums, totals)]


def kernel(
    nbr, lens, dq, dk, dv, cq, eq, ek, ev,
    self_out, cross_out,
    eqv, ekv, evv, cqv, halo, qf,
    stage, stat, of, co,
    qs, kf, vf, os_self, sc_buf, p_buf, tot_buf,
    idx_s, idx_all, idx_sm, row_tab, id_tab, req_tab,
    load_sem, z_send, z_recv, f_send, f_recv, y_send, y_recv, y_loc,
    q_send, q_recv, o_send, o_recv, t_send, t_recv, o_loc, t_loc, i_send, i_recv,
    b_send, b_recv, h_send, h_recv, e_send, e_recv, c_sem, misc,
    *chunked,
):
    kvs, pool, qb, os, ss, o_in, st_in, tail_s, tail_in = (
        chunked[n * CHUNKS : (n + 1) * CHUNKS] for n in range(9)
    )
    g = lax.axis_index("grp")
    s = lax.axis_index("seq")
    m = lax.axis_index("mp")
    z = lax.div(s, 2)
    core = lax.rem(s, 2)
    seq_len = lens[0]

    def z_dev(zz):
        return (g, 2 * zz + core, m)

    def y_dev(mm):
        return (g, s, mm)

    def x_dev(gg):
        return (gg, s, m)

    partner = (g, s + 1 - 2 * core, m)
    other = (g, mod(s + 15 + 2 * core, 16), m)
    behind = (g, mod(s + 15, 16), m)
    ahead = (g, mod(s + 1, 16), m)

    def remote(src, dst, send, recv, dev):
        return pltpu.make_async_remote_copy(
            src_ref=src, dst_ref=dst, send_sem=send, recv_sem=recv,
            device_id=dev, device_id_type=MESH,
        )

    loads = [
        pltpu.make_async_copy(src, dst, load_sem.at[n])
        for n, (src, dst) in enumerate(((cq.at[0], cqv), (eq, eqv), (ek, ekv), (ev, evv)))
    ]
    for c in loads:
        c.start()
    own = pl.ds(pl.multiple_of(z * HS, HS), HS)
    local_in = [
        pltpu.make_async_copy(dq.at[0, :, own], qs.at[z], load_sem.at[4]),
        pltpu.make_async_copy(dk.at[0, :, own], kf.at[core, z], load_sem.at[5]),
        pltpu.make_async_copy(dv.at[0, :, own], vf.at[core, z], load_sem.at[6]),
    ]
    for c in local_in:
        c.start()

    bar = pltpu.get_barrier_semaphore()
    peers = [z_dev(mod(z + off, 8)) for off in range(1, 8)]
    peers += [y_dev(mod(m + off, 4)) for off in range(1, 4)]
    peers += [x_dev(mod(g + off, 4)) for off in range(1, 4)]
    peers += [partner, other]
    for dev in peers:
        pl.semaphore_signal(bar, inc=1, device_id=dev, device_id_type=MESH)
    pl.semaphore_wait(bar, len(peers))

    halo_copy = remote(cq.at[0, pl.ds(0, SPAN)], halo, h_send.at[0], h_recv.at[0], behind)
    halo_copy.start()

    lane8 = lax.broadcasted_iota(jnp.int32, (8, 128), 1)
    packed = jnp.zeros((8, 128), jnp.int32)
    for n in range(8):
        packed = jnp.where(lane8 == n, nbr[0, n % 2, n // 2], packed)
    idx_s[...] = packed
    idx_copies = [
        remote(idx_s, idx_all.at[g], i_send.at[0], i_recv.at[0], x_dev(mod(g + off, 4)))
        for off in range(1, 4)
    ]
    for c in idx_copies:
        c.start()
    idx_local = pltpu.make_async_copy(idx_s, idx_all.at[g], misc.at[0])
    idx_local.start()

    z_order = (3, 5, 4, 2, 6, 1, 7)

    def both(ref, send, recv):
        return remote(ref, ref, send, recv, partner)

    def z_copy(off, part):
        zz = mod(z + off, 8)
        cols = pl.ds(pl.multiple_of(zz * HS, HS), HS)
        src = (dk, dq, dv)[part].at[0, :, cols]
        dst = (kf.at[core, z], qs.at[z], vf.at[core, z])[part]
        n = part if part < 2 else 1 + off
        return remote(src, dst, z_send.at[part], z_recv.at[n], z_dev(zz))

    def z_all(part):
        ref = (kf.at[core, pl.ds(0, 7)], qs.at[pl.ds(0, 7)], vf.at[core, pl.ds(0, 7)])[part]
        return both(ref, z_send.at[part], z_recv.at[part])

    def v_arrival(off):
        zz = mod(z + 8 - off, 8)
        ref = vf.at[core, zz]
        return remote(ref, ref, z_send.at[2], z_recv.at[1 + off], z_dev(zz))

    def v_forward(off):
        ref = vf.at[core, mod(z + 8 - off, 8)]
        return remote(ref, ref, f_send.at[1], f_recv.at[1], partner)

    def forward(part):
        ref = (kf, vf)[part].at[core]
        return remote(ref, ref, f_send.at[part], f_recv.at[part], partner)

    def forward_arrival(part):
        ref = (kf, vf)[part].at[1 - core]
        return remote(ref, ref, f_send.at[part], f_recv.at[part], partner)

    for part in range(3):
        for off in z_order:
            z_copy(off, part).start()

    def columns(hc):
        return slice(FIRST[hc] * HS, (FIRST[hc] + HEADS_OF[hc]) * HS)

    def y_copy(hc, off):
        return remote(
            kvs[hc].at[off], pool[hc].at[pl.ds(2 * m, 2)],
            y_send.at[hc], y_recv.at[hc], y_dev(mod(m + 1 + off, 4)),
        )

    def y_arrivals(hc):
        return both(pool[hc].at[pl.ds(0, 6)], y_send.at[hc], y_recv.at[hc])

    def y_local(hc):
        return pltpu.make_async_copy(kvs[hc].at[3], pool[hc].at[pl.ds(2 * m, 2)], y_loc.at[hc])

    def encode(hc):
        out = kvs[hc]

        def step(off, carry):
            t = mod(m + 1 + off, 4)
            tiles = [(n, j) for n in range(2) for j in range(HEADS_OF[hc])]
            cols = [
                pl.ds(pl.multiple_of((t * 8 + FIRST[hc] + j) * HS, HS), HS) for n, j in tiles
            ]
            q = [eqv[n, :, c] for (n, j), c in zip(tiles, cols)]
            k = [ekv[n, :, c] for (n, j), c in zip(tiles, cols)]
            v = [evv[n, :, c] for (n, j), c in zip(tiles, cols)]
            _, _, mixed = attend_all(q, k, v)
            for a, (n, j) in enumerate(tiles):
                at = slice(j * HS, (j + 1) * HS)
                out[off, n, 0, :, at] = (k[a].astype(F32) + mixed[a]).astype(BF16)
                out[off, n, 1, :, at] = (v[a].astype(F32) + mixed[a]).astype(BF16)

            @pl.when(off < 3)
            def _():
                y_copy(hc, off).start()

            @pl.when(off == 3)
            def _():
                y_local(hc).start()

            return carry

        lax.fori_loop(0, 4, step, 0)

    def q_copy(hc, off):
        mine = qb[hc].at[pl.ds(4 * g, 4)]
        return remote(
            mine, mine, q_send.at[hc], q_recv.at[hc], x_dev(mod(g + 1 + off, 4))
        )

    def q_arrivals(hc):
        return both(qb[hc].at[pl.ds(0, 12)], q_send.at[hc], q_recv.at[hc])

    def shift_queries():
        loads[0].wait()
        halo_copy.wait_recv()
        qf[0:ROWS, :] = cqv[...].astype(F32)
        qf[ROWS : ROWS + SPAN, :] = halo[...].astype(F32)
        for hc in range(CHUNKS):
            for u in range(4):
                first = SPAN - 1 + SPAN * u
                qb[hc][4 * g + u] = qf[first : first + SPAN, columns(hc)].astype(BF16)
            for off in range(3):
                q_copy(hc, off).start()

    def tables():
        both(idx_all.at[pl.ds(0, 3)], i_send.at[0], i_recv.at[0]).wait_recv()
        idx_local.wait()
        to_smem = pltpu.make_async_copy(idx_all, idx_sm, misc.at[1])
        to_smem.start()
        to_smem.wait()

        def per_candidate(c, carry):
            ids = [idx_sm[c, 0, n] for n in range(8)]
            count = jnp.int32(0)
            rows = [c * 4] * CAP
            locals_ = [jnp.int32(0)] * CAP
            for n in range(8):
                mine = lax.shift_right_logical(ids[n], 7) == g
                for r in range(CAP):
                    hit = jnp.logical_and(mine, count == r)
                    rows[r] = jnp.where(hit, c * 4 + n // 2, rows[r])
                    locals_[r] = jnp.where(hit, ids[n] & 7, locals_[r])
                count = count + jnp.where(mine, 1, 0)
            for r in range(CAP):
                row_tab[c * 4 + r] = rows[r]
                id_tab[c * 4 + r] = locals_[r]
            return carry

        lax.fori_loop(0, 4, per_candidate, 0)
        targets = [lax.shift_right_logical(nbr[0, n % 2, n // 2], 7) for n in range(8)]
        for n in range(8):
            rank = jnp.int32(0)
            for e in range(n):
                rank = rank + jnp.where(targets[e] == targets[n], 1, 0)
            req_tab[n] = targets[n] * CAP + rank

    lane64 = lax.broadcasted_iota(jnp.int32, (SPAN, 128), 1)

    def o_copy(hc, off):
        return remote(
            os[hc].at[off], o_in[hc].at[pl.ds(4 * g, 4)],
            o_send.at[hc], o_recv.at[hc], x_dev(mod(g + 1 + off, 4)),
        )

    def t_copy(hc, off):
        return remote(
            ss[hc].at[off], st_in[hc].at[g],
            t_send.at[hc], t_recv.at[hc], x_dev(mod(g + 1 + off, 4)),
        )

    def o_local(hc):
        return (
            pltpu.make_async_copy(
                os[hc].at[3], o_in[hc].at[pl.ds(4 * g, 4)], o_loc.at[hc]
            ),
            pltpu.make_async_copy(ss[hc].at[3], st_in[hc].at[g], t_loc.at[hc]),
        )

    def cross(hc):
        y_arrivals(hc).wait_recv()
        q_arrivals(hc).wait_recv()
        y_local(hc).wait()

        def step(off, carry):
            c = mod(g + 1 + off, 4)
            heads = range(HEADS_OF[hc])
            tiles = [(r, j) for r in range(CAP) for j in heads]
            q2 = [qb[hc][row_tab[c * 4 + r]] for r in range(CAP)]
            k2 = [pool[hc][id_tab[c * 4 + r], 0] for r in range(CAP)]
            v2 = [pool[hc][id_tab[c * 4 + r], 1] for r in range(CAP)]

            def split(x):
                return [x[r][:, j * HS : (j + 1) * HS] for r, j in tiles]

            tops, totals, mixed = attend_all(split(q2), split(k2), split(v2))
            logs = [top * SCALE + jnp.log2(total) for top, total in zip(tops, totals)]
            for a, (r, j) in enumerate(tiles):
                os[hc][off, r, :, j * HS : (j + 1) * HS] = mixed[a].astype(BF16)
            for r in range(CAP):
                row = jnp.where(lane64 == 0, logs[r * len(heads)], 0.0)
                for j in heads[1:]:
                    row = jnp.where(lane64 == j, logs[r * len(heads) + j], row)
                stage[r * SPAN : (r + 1) * SPAN, :] = row
            ss[hc][off] = jnp.transpose(stage[...])[0:8]

            @pl.when(off < 3)
            def _():
                o_copy(hc, off).start()
                t_copy(hc, off).start()

            @pl.when(off == 3)
            def _():
                for c_ in o_local(hc):
                    c_.start()

            return carry

        lax.fori_loop(0, 4, step, 0)

    def b_copy(i):
        return remote(
            os_self.at[i], self_out.at[0, :, own], b_send.at[0], b_recv.at[0], z_dev(i)
        )

    KEYS = 512
    key_iota = lax.broadcasted_iota(jnp.int32, (ROWS, KEYS), 1)
    row_iota = lax.broadcasted_iota(jnp.int32, (ROWS, KEYS), 0)

    def self_weights():
        for i in reversed(range(8)):
            q = qs[i]
            top = None
            for j in range(i + 1):
                sc = scores_of(q, jnp.concatenate([kf[0, j], kf[1, j]], axis=0))
                if j == i:
                    sc = jnp.where(key_iota <= row_iota + core * ROWS, sc, MASKED)
                sc_buf[j] = sc
                high = fold(sc, jnp.maximum)
                top = high if top is None else jnp.maximum(top, high)
            top = jnp.max(top, axis=1, keepdims=True) * SCALE
            total = None
            for j in range(i + 1):
                w = jnp.exp2(sc_buf[j] * SCALE - top)
                for half in range(2):
                    p_buf[i, half, :, j * ROWS : (j + 1) * ROWS] = w[
                        :, half * ROWS : (half + 1) * ROWS
                    ].astype(BF16)
                low = fold(w, jnp.add)
                total = low if total is None else total + low
            tot_buf[i] = total

    def values_part(i, half):
        return jnp.dot(
            p_buf[i, half, :, 0 : (i + 1) * ROWS],
            vf[half, 0 : i + 1].reshape((i + 1) * ROWS, HS),
            preferred_element_type=F32,
        )

    def self_values():
        for i in reversed(range(8)):
            sc_buf[i, :, 0:HS] = values_part(i, core)
        forward_arrival(1).wait_recv()
        for i in reversed(range(8)):
            acc = sc_buf[i, :, 0:HS] + values_part(i, 1 - core)
            total = jnp.sum(tot_buf[i], axis=1, keepdims=True)
            pos = (2 * i + core) * ROWS + lax.broadcasted_iota(jnp.int32, (ROWS, HS), 0)
            os_self[i] = jnp.where(pos < seq_len, acc * (1.0 / total), 0.0).astype(BF16)
        for off in z_order:
            b_copy(mod(z + off, 8)).start()
        pltpu.make_async_copy(os_self.at[z], self_out.at[0, :, own], misc.at[10]).start()

    first_pos = s * ROWS

    def o_arrivals(hc):
        both(o_in[hc].at[pl.ds(0, 12)], o_send.at[hc], o_recv.at[hc]).wait_recv()
        both(st_in[hc].at[pl.ds(0, 3)], t_send.at[hc], t_recv.at[hc]).wait_recv()
        for c in o_local(hc):
            c.wait()

    def tail_copy(hc):
        return remote(tail_s[hc], tail_in[hc], e_send.at[hc], e_recv.at[hc], ahead)

    def out_copy(hc):
        return pltpu.make_async_copy(
            co.at[:, columns(hc)], cross_out.at[0, :, columns(hc)], c_sem.at[hc]
        )

    def live(first, rows, width):
        pos = first_pos + first + lax.broadcasted_iota(jnp.int32, (rows, width), 0)
        return jnp.logical_and(pos >= SPAN - 1, pos < seq_len)

    def combine(hc):
        width = HEADS_OF[hc] * HS
        cols = columns(hc)
        o_arrivals(hc)
        logs = jnp.concatenate([st_in[hc][...].reshape(32, 256), jnp.zeros((96, 256), F32)], axis=0)
        turned = jnp.transpose(logs)
        for gg in range(4):
            part = turned if gg == 0 else pltpu.roll(turned, 128 - 8 * gg, 1)
            for r in range(CAP):
                stat[gg * CAP + r] = part[r * SPAN : (r + 1) * SPAN, :]
        of[ROWS + 56 : ROWS + 64, cols] = jnp.zeros((8, width), F32)
        for u in (3, 0, 1, 2):
            s0, s1 = req_tab[2 * u], req_tab[2 * u + 1]
            l0, l1 = stat[s0], stat[s1]
            top = jnp.maximum(l0, l1)
            w0, w1 = jnp.exp2(l0 - top), jnp.exp2(l1 - top)
            inv = 1.0 / (w0 + w1)
            w0, w1 = w0 * inv, w1 * inv
            o0, o1 = o_in[hc][s0], o_in[hc][s1]
            first = SPAN - 1 + SPAN * u
            for j in range(HEADS_OF[hc]):
                at = slice(j * HS, (j + 1) * HS)
                of[first : first + SPAN, cols.start + j * HS : cols.start + (j + 1) * HS] = (
                    o0[:, at].astype(F32) * w0[:, j : j + 1]
                    + o1[:, at].astype(F32) * w1[:, j : j + 1]
                )
            if u == 3:
                tail_s[hc][...] = of[ROWS : ROWS + SPAN, cols].astype(BF16)
                tail_copy(hc).start()
        co[SPAN:ROWS, cols] = jnp.where(
            live(SPAN, ROWS - SPAN, width), of[SPAN:ROWS, cols], 0.0
        ).astype(BF16)

    def finish(hc):
        width = HEADS_OF[hc] * HS
        cols = columns(hc)
        tail_copy(hc).wait_recv()
        row = lax.broadcasted_iota(jnp.int32, (SPAN, width), 0)
        head = jnp.where(row < SPAN - 1, tail_in[hc][...].astype(F32), of[0:SPAN, cols])
        co[0:SPAN, cols] = jnp.where(live(0, SPAN, width), head, 0.0).astype(BF16)
        out_copy(hc).start()

    def sent(hc):
        both(kvs[hc].at[pl.ds(0, 3)], y_send.at[hc], y_recv.at[hc]).wait_send()
        q_arrivals(hc).wait_send()

    def answered(hc):
        both(os[hc].at[pl.ds(0, 3)], o_send.at[hc], o_recv.at[hc]).wait_send()
        both(ss[hc].at[pl.ds(0, 3)], t_send.at[hc], t_recv.at[hc]).wait_send()
        tail_copy(hc).wait_send()

    for c in loads[1:]:
        c.wait()
    encode(0)
    shift_queries()
    for hc in range(1, CHUNKS):
        encode(hc)
    for c in local_in:
        c.wait()
    tables()
    cross(0)
    z_all(0).wait_recv()
    forward(0).start()
    v_forward(0).start()
    halo_copy.wait_send()
    both(idx_all.at[pl.ds(0, 3)], i_send.at[0], i_recv.at[0]).wait_send()
    cross(1)
    sent(0)
    z_all(1).wait_recv()
    forward_arrival(0).wait_recv()
    self_weights()
    cross(2)
    for off in z_order:
        v_arrival(off).wait_recv()
        v_forward(off).start()
    sent(1)
    for part in range(3):
        z_all(part).wait_send()
    combine(0)
    self_values()
    cross(3)
    combine(1)
    cross(4)
    sent(2)
    sent(3)
    sent(4)
    for part in range(2):
        forward(part).wait_send()
    combine(2)
    combine(3)
    combine(4)
    answered(0)
    answered(1)
    finish(0)
    finish(1)
    finish(2)
    finish(3)
    finish(4)
    answered(2)
    answered(3)
    answered(4)

    pltpu.make_async_copy(os_self.at[z], self_out.at[0, :, own], misc.at[10]).wait()
    both(self_out.at[0, :, pl.ds(0, 7 * HS)], b_send.at[0], b_recv.at[0]).wait_recv()
    both(os_self.at[pl.ds(0, 7)], b_send.at[0], b_recv.at[0]).wait_send()
    for hc in range(CHUNKS):
        out_copy(hc).wait()


def place(a_ref, b_ref, a_out, b_out, held, in_sem, out_sem):
    pieces = [
        (src.at[0, pl.ds(half * 128, 128)], dst.at[0, pl.ds(half * 128, 128)])
        for half in range(2)
        for src, dst in ((a_ref, a_out), (b_ref, b_out))
    ]
    loads = [
        pltpu.make_async_copy(src, held.at[n], in_sem.at[n]) for n, (src, _) in enumerate(pieces)
    ]
    stores = [
        pltpu.make_async_copy(held.at[n], dst, out_sem.at[n]) for n, (_, dst) in enumerate(pieces)
    ]
    for c in loads:
        c.start()
    for load, store in zip(loads, stores):
        load.wait()
        store.start()
    for c in stores:
        c.wait()


def local(*args):
    dec_query, dec_key, dec_value, cross_query, enc_query, enc_key, enc_value, nbr_index, seq_lengths = args
    any_ = pl.BlockSpec(memory_space=pl.ANY)
    smem = pl.BlockSpec(memory_space=pltpu.SMEM)
    V = pltpu.VMEM
    dma = lambda n: pltpu.SemaphoreType.DMA((n,))
    scratch = [V((2, 128, 4096), BF16)] * 3
    scratch += [V((ROWS, WIDTH), BF16), V((SPAN, WIDTH), BF16), V((ROWS + SPAN, WIDTH), F32)]
    scratch += [
        V((256, 128), F32), V((16, SPAN, 128), F32), V((ROWS + SPAN, WIDTH), F32),
        V((ROWS, WIDTH), BF16),
    ]
    scratch += [
        V((8, ROWS, HS), BF16), V((2, 8, ROWS, HS), BF16), V((2, 8, ROWS, HS), BF16),
        V((8, ROWS, HS), BF16), V((8, ROWS, 512), F32), V((8, 2, ROWS, 2048), BF16), V((8, ROWS, HS), F32),
    ]
    scratch += [
        V((8, 128), jnp.int32), V((4, 8, 128), jnp.int32), pltpu.SMEM((4, 8, 128), jnp.int32),
        pltpu.SMEM((16,), jnp.int32), pltpu.SMEM((16,), jnp.int32), pltpu.SMEM((8,), jnp.int32),
    ]
    scratch += [
        dma(n)
        for n in (
            7, 3, 9, 2, 2, CHUNKS, CHUNKS, CHUNKS, CHUNKS, CHUNKS, CHUNKS, CHUNKS, CHUNKS, CHUNKS,
            CHUNKS, CHUNKS, 1, 1, 1, 1, 1, 1, CHUNKS, CHUNKS, CHUNKS, 12,
        )
    ]
    widths = [n * HS for n in HEADS_OF]
    for form in (
        lambda w: V((4, 2, 2, 128, w), BF16),
        lambda w: V((8, 2, 128, w), BF16),
        lambda w: V((16, SPAN, w), BF16),
        lambda w: V((4, 4, SPAN, w), BF16),
        lambda w: V((4, 8, 256), F32),
        lambda w: V((16, SPAN, w), BF16),
        lambda w: V((4, 8, 256), F32),
        lambda w: V((SPAN, w), BF16),
        lambda w: V((SPAN, w), BF16),
    ):
        scratch += [form(w) for w in widths]
    shape = jax.ShapeDtypeStruct((1, ROWS, WIDTH), BF16)
    both = pl.pallas_call(
        kernel,
        out_shape=(shape, shape),
        in_specs=[smem, smem] + [any_] * 7,
        out_specs=(any_, any_),
        scratch_shapes=scratch,
        compiler_params=pltpu.CompilerParams(
            collective_id=0, has_side_effects=True, vmem_limit_bytes=56 << 20
        ),
        name="retro_block",
    )(jnp.transpose(nbr_index, (0, 2, 1)), seq_lengths, dec_query, dec_key, dec_value, cross_query, enc_query, enc_key, enc_value)
    return pl.pallas_call(
        place,
        out_shape=(shape, shape),
        in_specs=[any_] * 2,
        out_specs=(any_, any_),
        scratch_shapes=[V((4, 128, WIDTH), BF16), dma(4), dma(4)],
        name="place",
    )(*both)


def solution(mesh):
    rows = P("grp", "seq", "mp")
    store = P(("grp", "seq", "mp"), None, None)
    return jax.shard_map(
        local,
        mesh=mesh,
        in_specs=(rows, rows, rows, rows, store, store, store, P("grp", "seq", None), P("grp")),
        out_specs=(rows, rows),
        check_vma=False,
    )
```

```python
import functools
import math

import jax
import jax.numpy as jnp
from jax import lax
from jax.experimental import pallas as pl
from jax.experimental.pallas import tpu as pltpu
from jax.sharding import PartitionSpec as P

HS = 128
SPAN = 64
CAP = 4
HEADS_OF = (1, 2, 2, 1, 1, 1)
FIRST = (0, 1, 3, 5, 6, 7)
CHUNKS = len(HEADS_OF)
ROWS = 256
WIDTH = 1024
SCALE = HS ** (-0.5) * math.log2(math.e)
MASKED = -1e30
MESH = pl.DeviceIdType.MESH
F32 = jnp.float32
BF16 = jnp.bfloat16
NT = (((1,), (1,)), ((), ()))


def mod(a, n):
    return lax.rem(a, n)


def scores_of(q, k):
    return lax.dot_general(q, k, NT, preferred_element_type=F32)


def mix(weights, v):
    return jnp.dot(weights.astype(BF16), v, preferred_element_type=F32)


def fold(x, op):
    parts = [x[:, a : a + HS] for a in range(0, x.shape[1], HS)]
    while len(parts) > 1:
        parts = [op(parts[a], parts[a + 1]) for a in range(0, len(parts), 2)]
    return parts[0]


def attend_all(queries, keys, values):
    scores = [scores_of(q, k) for q, k in zip(queries, keys)]
    tops = [jnp.max(x, axis=1, keepdims=True) for x in scores]
    weights = [jnp.exp2((x - top) * SCALE) for x, top in zip(scores, tops)]
    totals = [jnp.sum(w, axis=1, keepdims=True) for w in weights]
    sums = [mix(w, v) for w, v in zip(weights, values)]
    return tops, totals, [x * (1.0 / total) for x, total in zip(sums, totals)]


def kernel(
    nbr, lens, dq, dk, dv, cq, eq, ek, ev,
    self_out, cross_out,
    eqv, ekv, evv, cqv, halo, qf,
    stage, stat, of, co,
    qs, kf, vf, os_self, sc_buf, p_buf, tot_buf,
    idx_s, idx_all, idx_sm, row_tab, id_tab, req_tab,
    load_sem, z_send, z_recv, f_send, f_recv, y_send, y_recv, y_loc,
    q_send, q_recv, o_send, o_recv, t_send, t_recv, o_loc, t_loc, i_send, i_recv,
    b_send, b_recv, h_send, h_recv, e_send, e_recv, c_sem, misc,
    *chunked,
):
    kvs, pool, qb, os, ss, o_in, st_in, tail_s, tail_in = (
        chunked[n * CHUNKS : (n + 1) * CHUNKS] for n in range(9)
    )
    g = lax.axis_index("grp")
    s = lax.axis_index("seq")
    m = lax.axis_index("mp")
    z = lax.div(s, 2)
    core = lax.rem(s, 2)
    seq_len = lens[0]

    def z_dev(zz):
        return (g, 2 * zz + core, m)

    def y_dev(mm):
        return (g, s, mm)

    def x_dev(gg):
        return (gg, s, m)

    partner = (g, s + 1 - 2 * core, m)
    other = (g, mod(s + 15 + 2 * core, 16), m)
    behind = (g, mod(s + 15, 16), m)
    ahead = (g, mod(s + 1, 16), m)

    def remote(src, dst, send, recv, dev):
        return pltpu.make_async_remote_copy(
            src_ref=src, dst_ref=dst, send_sem=send, recv_sem=recv,
            device_id=dev, device_id_type=MESH,
        )

    loads = [
        pltpu.make_async_copy(src, dst, load_sem.at[n])
        for n, (src, dst) in enumerate(((cq.at[0], cqv), (eq, eqv), (ek, ekv), (ev, evv)))
    ]
    for c in loads:
        c.start()
    own = pl.ds(pl.multiple_of(z * HS, HS), HS)
    local_in = [
        pltpu.make_async_copy(dq.at[0, :, own], qs.at[z], load_sem.at[4]),
        pltpu.make_async_copy(dk.at[0, :, own], kf.at[core, z], load_sem.at[5]),
        pltpu.make_async_copy(dv.at[0, :, own], vf.at[core, z], load_sem.at[6]),
    ]
    for c in local_in:
        c.start()

    bar = pltpu.get_barrier_semaphore()
    peers = [z_dev(mod(z + off, 8)) for off in range(1, 8)]
    peers += [y_dev(mod(m + off, 4)) for off in range(1, 4)]
    peers += [x_dev(mod(g + off, 4)) for off in range(1, 4)]
    peers += [partner, other]
    for dev in peers:
        pl.semaphore_signal(bar, inc=1, device_id=dev, device_id_type=MESH)
    pl.semaphore_wait(bar, len(peers))

    halo_copy = remote(cq.at[0, pl.ds(0, SPAN)], halo, h_send.at[0], h_recv.at[0], behind)
    halo_copy.start()

    lane8 = lax.broadcasted_iota(jnp.int32, (8, 128), 1)
    packed = jnp.zeros((8, 128), jnp.int32)
    for n in range(8):
        packed = jnp.where(lane8 == n, nbr[0, n % 2, n // 2], packed)
    idx_s[...] = packed
    idx_copies = [
        remote(idx_s, idx_all.at[g], i_send.at[0], i_recv.at[0], x_dev(mod(g + off, 4)))
        for off in range(1, 4)
    ]
    for c in idx_copies:
        c.start()
    idx_local = pltpu.make_async_copy(idx_s, idx_all.at[g], misc.at[0])
    idx_local.start()

    z_order = (3, 5, 4, 2, 6, 1, 7)

    def both(ref, send, recv):
        return remote(ref, ref, send, recv, partner)

    def z_copy(off, part):
        zz = mod(z + off, 8)
        cols = pl.ds(pl.multiple_of(zz * HS, HS), HS)
        src = (dk, dq, dv)[part].at[0, :, cols]
        dst = (kf.at[core, z], qs.at[z], vf.at[core, z])[part]
        n = part if part < 2 else 1 + off
        return remote(src, dst, z_send.at[part], z_recv.at[n], z_dev(zz))

    def z_all(part):
        ref = (kf.at[core, pl.ds(0, 7)], qs.at[pl.ds(0, 7)], vf.at[core, pl.ds(0, 7)])[part]
        return both(ref, z_send.at[part], z_recv.at[part])

    def v_arrival(off):
        zz = mod(z + 8 - off, 8)
        ref = vf.at[core, zz]
        return remote(ref, ref, z_send.at[2], z_recv.at[1 + off], z_dev(zz))

    def v_forward(off):
        ref = vf.at[core, mod(z + 8 - off, 8)]
        return remote(ref, ref, f_send.at[1], f_recv.at[1], partner)

    def forward(part):
        ref = (kf, vf)[part].at[core]
        return remote(ref, ref, f_send.at[part], f_recv.at[part], partner)

    def forward_arrival(part):
        ref = (kf, vf)[part].at[1 - core]
        return remote(ref, ref, f_send.at[part], f_recv.at[part], partner)

    for off in z_order:
        z_copy(off, 0).start()

    def columns(hc):
        return slice(FIRST[hc] * HS, (FIRST[hc] + HEADS_OF[hc]) * HS)

    def y_copy(hc, off):
        return remote(
            kvs[hc].at[off], pool[hc].at[pl.ds(2 * m, 2)],
            y_send.at[hc], y_recv.at[hc], y_dev(mod(m + 1 + off, 4)),
        )

    def y_arrivals(hc):
        return both(pool[hc].at[pl.ds(0, 6)], y_send.at[hc], y_recv.at[hc])

    def y_local(hc):
        return pltpu.make_async_copy(kvs[hc].at[3], pool[hc].at[pl.ds(2 * m, 2)], y_loc.at[hc])

    def encode(hc):
        out = kvs[hc]

        def step(off, carry):
            t = mod(m + 1 + off, 4)
            tiles = [(n, j) for n in range(2) for j in range(HEADS_OF[hc])]
            cols = [
                pl.ds(pl.multiple_of((t * 8 + FIRST[hc] + j) * HS, HS), HS) for n, j in tiles
            ]
            q = [eqv[n, :, c] for (n, j), c in zip(tiles, cols)]
            k = [ekv[n, :, c] for (n, j), c in zip(tiles, cols)]
            v = [evv[n, :, c] for (n, j), c in zip(tiles, cols)]
            _, _, mixed = attend_all(q, k, v)
            for a, (n, j) in enumerate(tiles):
                at = slice(j * HS, (j + 1) * HS)
                out[off, n, 0, :, at] = (k[a].astype(F32) + mixed[a]).astype(BF16)
                out[off, n, 1, :, at] = (v[a].astype(F32) + mixed[a]).astype(BF16)

            @pl.when(off < 3)
            def _():
                y_copy(hc, off).start()

            @pl.when(off == 3)
            def _():
                y_local(hc).start()

            return carry

        lax.fori_loop(0, 4, step, 0)

    def q_copy(hc, off):
        mine = qb[hc].at[pl.ds(4 * g, 4)]
        return remote(
            mine, mine, q_send.at[hc], q_recv.at[hc], x_dev(mod(g + 1 + off, 4))
        )

    def q_arrivals(hc):
        return both(qb[hc].at[pl.ds(0, 12)], q_send.at[hc], q_recv.at[hc])

    def shift_queries():
        loads[0].wait()
        halo_copy.wait_recv()
        qf[0:ROWS, :] = cqv[...].astype(F32)
        qf[ROWS : ROWS + SPAN, :] = halo[...].astype(F32)
        for hc in range(CHUNKS):
            for u in range(4):
                first = SPAN - 1 + SPAN * u
                qb[hc][4 * g + u] = qf[first : first + SPAN, columns(hc)].astype(BF16)
            for off in range(3):
                q_copy(hc, off).start()

    def tables():
        both(idx_all.at[pl.ds(0, 3)], i_send.at[0], i_recv.at[0]).wait_recv()
        idx_local.wait()
        to_smem = pltpu.make_async_copy(idx_all, idx_sm, misc.at[1])
        to_smem.start()
        to_smem.wait()

        def per_candidate(c, carry):
            ids = [idx_sm[c, 0, n] for n in range(8)]
            count = jnp.int32(0)
            rows = [c * 4] * CAP
            locals_ = [jnp.int32(0)] * CAP
            for n in range(8):
                mine = lax.shift_right_logical(ids[n], 7) == g
                for r in range(CAP):
                    hit = jnp.logical_and(mine, count == r)
                    rows[r] = jnp.where(hit, c * 4 + n // 2, rows[r])
                    locals_[r] = jnp.where(hit, ids[n] & 7, locals_[r])
                count = count + jnp.where(mine, 1, 0)
            for r in range(CAP):
                row_tab[c * 4 + r] = rows[r]
                id_tab[c * 4 + r] = locals_[r]
            return carry

        lax.fori_loop(0, 4, per_candidate, 0)
        targets = [lax.shift_right_logical(nbr[0, n % 2, n // 2], 7) for n in range(8)]
        for n in range(8):
            rank = jnp.int32(0)
            for e in range(n):
                rank = rank + jnp.where(targets[e] == targets[n], 1, 0)
            req_tab[n] = targets[n] * CAP + rank

    lane64 = lax.broadcasted_iota(jnp.int32, (SPAN, 128), 1)

    def o_copy(hc, off):
        return remote(
            os[hc].at[off], o_in[hc].at[pl.ds(4 * g, 4)],
            o_send.at[hc], o_recv.at[hc], x_dev(mod(g + 1 + off, 4)),
        )

    def t_copy(hc, off):
        return remote(
            ss[hc].at[off], st_in[hc].at[g],
            t_send.at[hc], t_recv.at[hc], x_dev(mod(g + 1 + off, 4)),
        )

    def o_local(hc):
        return (
            pltpu.make_async_copy(
                os[hc].at[3], o_in[hc].at[pl.ds(4 * g, 4)], o_loc.at[hc]
            ),
            pltpu.make_async_copy(ss[hc].at[3], st_in[hc].at[g], t_loc.at[hc]),
        )

    def cross(hc):
        y_arrivals(hc).wait_recv()
        q_arrivals(hc).wait_recv()
        y_local(hc).wait()

        heads = range(HEADS_OF[hc])
        group = 2 if len(heads) == 1 else 1

        def step(turn, carry):
            tiles = [(a, r, j) for a in range(group) for r in range(CAP) for j in heads]
            offs = [turn * group + a for a in range(group)]
            cands = [mod(g + 1 + off, 4) for off in offs]
            q2 = [[qb[hc][row_tab[c * 4 + r]] for r in range(CAP)] for c in cands]
            k2 = [[pool[hc][id_tab[c * 4 + r], 0] for r in range(CAP)] for c in cands]
            v2 = [[pool[hc][id_tab[c * 4 + r], 1] for r in range(CAP)] for c in cands]

            def split(x):
                return [x[a][r][:, j * HS : (j + 1) * HS] for a, r, j in tiles]

            tops, totals, mixed = attend_all(split(q2), split(k2), split(v2))
            logs = [top * SCALE + jnp.log2(total) for top, total in zip(tops, totals)]
            for n, (a, r, j) in enumerate(tiles):
                os[hc][offs[a], r, :, j * HS : (j + 1) * HS] = mixed[n].astype(BF16)
            for a, off in enumerate(offs):
                for r in range(CAP):
                    base = (a * CAP + r) * len(heads)
                    row = jnp.where(lane64 == 0, logs[base], 0.0)
                    for j in heads[1:]:
                        row = jnp.where(lane64 == j, logs[base + j], row)
                    stage[r * SPAN : (r + 1) * SPAN, :] = row
                ss[hc][off] = jnp.transpose(stage[...])[0:8]
                answer(off)
            return carry

        def answer(off):
            @pl.when(off < 3)
            def _():
                o_copy(hc, off).start()
                t_copy(hc, off).start()

            @pl.when(off == 3)
            def _():
                for c_ in o_local(hc):
                    c_.start()

        lax.fori_loop(0, 4 // group, step, 0)

    def b_copy(i):
        return remote(
            os_self.at[i], self_out.at[0, :, own], b_send.at[0], b_recv.at[0], z_dev(i)
        )

    KEYS = 512
    key_iota = lax.broadcasted_iota(jnp.int32, (ROWS, KEYS), 1)
    row_iota = lax.broadcasted_iota(jnp.int32, (ROWS, KEYS), 0)

    def self_weights():
        for i in reversed(range(8)):
            q = qs[i]
            top = None
            for j in range(i + 1):
                sc = scores_of(q, jnp.concatenate([kf[0, j], kf[1, j]], axis=0))
                if j == i:
                    sc = jnp.where(key_iota <= row_iota + core * ROWS, sc, MASKED)
                sc_buf[j] = sc
                high = fold(sc, jnp.maximum)
                top = high if top is None else jnp.maximum(top, high)
            top = jnp.max(top, axis=1, keepdims=True) * SCALE
            total = None
            for j in range(i + 1):
                w = jnp.exp2(sc_buf[j] * SCALE - top)
                for half in range(2):
                    p_buf[i, half, :, j * ROWS : (j + 1) * ROWS] = w[
                        :, half * ROWS : (half + 1) * ROWS
                    ].astype(BF16)
                low = fold(w, jnp.add)
                total = low if total is None else total + low
            tot_buf[i] = total

    def values_part(i, half):
        return jnp.dot(
            p_buf[i, half, :, 0 : (i + 1) * ROWS],
            vf[half, 0 : i + 1].reshape((i + 1) * ROWS, HS),
            preferred_element_type=F32,
        )

    def self_values():
        for i in reversed(range(8)):
            sc_buf[i, :, 0:HS] = values_part(i, core)
        forward_arrival(1).wait_recv()
        for i in reversed(range(8)):
            acc = sc_buf[i, :, 0:HS] + values_part(i, 1 - core)
            total = jnp.sum(tot_buf[i], axis=1, keepdims=True)
            pos = (2 * i + core) * ROWS + lax.broadcasted_iota(jnp.int32, (ROWS, HS), 0)
            os_self[i] = jnp.where(pos < seq_len, acc * (1.0 / total), 0.0).astype(BF16)
        for off in z_order:
            b_copy(mod(z + off, 8)).start()
        pltpu.make_async_copy(os_self.at[z], self_out.at[0, :, own], misc.at[10]).start()

    first_pos = s * ROWS

    def o_arrivals(hc):
        both(o_in[hc].at[pl.ds(0, 12)], o_send.at[hc], o_recv.at[hc]).wait_recv()
        both(st_in[hc].at[pl.ds(0, 3)], t_send.at[hc], t_recv.at[hc]).wait_recv()
        for c in o_local(hc):
            c.wait()

    def tail_copy(hc):
        return remote(tail_s[hc], tail_in[hc], e_send.at[hc], e_recv.at[hc], ahead)

    def out_copy(hc):
        return pltpu.make_async_copy(
            co.at[:, columns(hc)], cross_out.at[0, :, columns(hc)], c_sem.at[hc]
        )

    def live(first, rows, width):
        pos = first_pos + first + lax.broadcasted_iota(jnp.int32, (rows, width), 0)
        return jnp.logical_and(pos >= SPAN - 1, pos < seq_len)

    def combine(hc):
        width = HEADS_OF[hc] * HS
        cols = columns(hc)
        o_arrivals(hc)
        logs = jnp.concatenate([st_in[hc][...].reshape(32, 256), jnp.zeros((96, 256), F32)], axis=0)
        turned = jnp.transpose(logs)
        for gg in range(4):
            part = turned if gg == 0 else pltpu.roll(turned, 128 - 8 * gg, 1)
            for r in range(CAP):
                stat[gg * CAP + r] = part[r * SPAN : (r + 1) * SPAN, :]
        of[ROWS + 56 : ROWS + 64, cols] = jnp.zeros((8, width), F32)
        for u in (3, 0, 1, 2):
            s0, s1 = req_tab[2 * u], req_tab[2 * u + 1]
            l0, l1 = stat[s0], stat[s1]
            top = jnp.maximum(l0, l1)
            w0, w1 = jnp.exp2(l0 - top), jnp.exp2(l1 - top)
            inv = 1.0 / (w0 + w1)
            w0, w1 = w0 * inv, w1 * inv
            o0, o1 = o_in[hc][s0], o_in[hc][s1]
            first = SPAN - 1 + SPAN * u
            for j in range(HEADS_OF[hc]):
                at = slice(j * HS, (j + 1) * HS)
                of[first : first + SPAN, cols.start + j * HS : cols.start + (j + 1) * HS] = (
                    o0[:, at].astype(F32) * w0[:, j : j + 1]
                    + o1[:, at].astype(F32) * w1[:, j : j + 1]
                )
            if u == 3:
                tail_s[hc][...] = of[ROWS : ROWS + SPAN, cols].astype(BF16)
                tail_copy(hc).start()
        co[SPAN:ROWS, cols] = jnp.where(
            live(SPAN, ROWS - SPAN, width), of[SPAN:ROWS, cols], 0.0
        ).astype(BF16)

    def finish(hc):
        width = HEADS_OF[hc] * HS
        cols = columns(hc)
        tail_copy(hc).wait_recv()
        row = lax.broadcasted_iota(jnp.int32, (SPAN, width), 0)
        head = jnp.where(row < SPAN - 1, tail_in[hc][...].astype(F32), of[0:SPAN, cols])
        co[0:SPAN, cols] = jnp.where(live(0, SPAN, width), head, 0.0).astype(BF16)
        out_copy(hc).start()

    def sent(hc):
        both(kvs[hc].at[pl.ds(0, 3)], y_send.at[hc], y_recv.at[hc]).wait_send()
        q_arrivals(hc).wait_send()

    def answered(hc):
        both(os[hc].at[pl.ds(0, 3)], o_send.at[hc], o_recv.at[hc]).wait_send()
        both(ss[hc].at[pl.ds(0, 3)], t_send.at[hc], t_recv.at[hc]).wait_send()
        tail_copy(hc).wait_send()

    for c in loads[1:]:
        c.wait()
    encode(0)
    for part in (1, 2):
        for off in z_order:
            z_copy(off, part).start()
    shift_queries()
    for hc in range(1, CHUNKS):
        encode(hc)
    for c in local_in:
        c.wait()
    tables()
    cross(0)
    z_all(0).wait_recv()
    forward(0).start()
    v_forward(0).start()
    halo_copy.wait_send()
    both(idx_all.at[pl.ds(0, 3)], i_send.at[0], i_recv.at[0]).wait_send()
    cross(1)
    sent(0)
    z_all(1).wait_recv()
    forward_arrival(0).wait_recv()
    self_weights()
    cross(2)
    for off in z_order:
        v_arrival(off).wait_recv()
        v_forward(off).start()
    sent(1)
    for part in range(3):
        z_all(part).wait_send()
    combine(0)
    self_values()
    cross(3)
    combine(1)
    cross(4)
    combine(2)
    cross(5)
    sent(2)
    sent(3)
    sent(4)
    sent(5)
    for part in range(2):
        forward(part).wait_send()
    combine(3)
    combine(4)
    combine(5)
    answered(0)
    answered(1)
    finish(0)
    finish(1)
    finish(2)
    finish(3)
    finish(4)
    finish(5)
    answered(2)
    answered(3)
    answered(4)
    answered(5)

    pltpu.make_async_copy(os_self.at[z], self_out.at[0, :, own], misc.at[10]).wait()
    both(self_out.at[0, :, pl.ds(0, 7 * HS)], b_send.at[0], b_recv.at[0]).wait_recv()
    both(os_self.at[pl.ds(0, 7)], b_send.at[0], b_recv.at[0]).wait_send()
    for hc in range(CHUNKS):
        out_copy(hc).wait()


def place(a_ref, b_ref, a_out, b_out, held, in_sem, out_sem):
    pieces = [
        (src.at[0, pl.ds(half * 128, 128)], dst.at[0, pl.ds(half * 128, 128)])
        for half in range(2)
        for src, dst in ((a_ref, a_out), (b_ref, b_out))
    ]
    loads = [
        pltpu.make_async_copy(src, held.at[n], in_sem.at[n]) for n, (src, _) in enumerate(pieces)
    ]
    stores = [
        pltpu.make_async_copy(held.at[n], dst, out_sem.at[n]) for n, (_, dst) in enumerate(pieces)
    ]
    for c in loads:
        c.start()
    for load, store in zip(loads, stores):
        load.wait()
        store.start()
    for c in stores:
        c.wait()


def local(*args):
    dec_query, dec_key, dec_value, cross_query, enc_query, enc_key, enc_value, nbr_index, seq_lengths = args
    any_ = pl.BlockSpec(memory_space=pl.ANY)
    smem = pl.BlockSpec(memory_space=pltpu.SMEM)
    V = pltpu.VMEM
    dma = lambda n: pltpu.SemaphoreType.DMA((n,))
    scratch = [V((2, 128, 4096), BF16)] * 3
    scratch += [V((ROWS, WIDTH), BF16), V((SPAN, WIDTH), BF16), V((ROWS + SPAN, WIDTH), F32)]
    scratch += [
        V((256, 128), F32), V((16, SPAN, 128), F32), V((ROWS + SPAN, WIDTH), F32),
        V((ROWS, WIDTH), BF16),
    ]
    scratch += [
        V((8, ROWS, HS), BF16), V((2, 8, ROWS, HS), BF16), V((2, 8, ROWS, HS), BF16),
        V((8, ROWS, HS), BF16), V((8, ROWS, 512), F32), V((8, 2, ROWS, 2048), BF16), V((8, ROWS, HS), F32),
    ]
    scratch += [
        V((8, 128), jnp.int32), V((4, 8, 128), jnp.int32), pltpu.SMEM((4, 8, 128), jnp.int32),
        pltpu.SMEM((16,), jnp.int32), pltpu.SMEM((16,), jnp.int32), pltpu.SMEM((8,), jnp.int32),
    ]
    scratch += [
        dma(n)
        for n in (
            7, 3, 9, 2, 2, CHUNKS, CHUNKS, CHUNKS, CHUNKS, CHUNKS, CHUNKS, CHUNKS, CHUNKS, CHUNKS,
            CHUNKS, CHUNKS, 1, 1, 1, 1, 1, 1, CHUNKS, CHUNKS, CHUNKS, 12,
        )
    ]
    widths = [n * HS for n in HEADS_OF]
    for form in (
        lambda w: V((4, 2, 2, 128, w), BF16),
        lambda w: V((8, 2, 128, w), BF16),
        lambda w: V((16, SPAN, w), BF16),
        lambda w: V((4, 4, SPAN, w), BF16),
        lambda w: V((4, 8, 256), F32),
        lambda w: V((16, SPAN, w), BF16),
        lambda w: V((4, 8, 256), F32),
        lambda w: V((SPAN, w), BF16),
        lambda w: V((SPAN, w), BF16),
    ):
        scratch += [form(w) for w in widths]
    shape = jax.ShapeDtypeStruct((1, ROWS, WIDTH), BF16)
    both = pl.pallas_call(
        kernel,
        out_shape=(shape, shape),
        in_specs=[smem, smem] + [any_] * 7,
        out_specs=(any_, any_),
        scratch_shapes=scratch,
        compiler_params=pltpu.CompilerParams(
            collective_id=0, has_side_effects=True, vmem_limit_bytes=56 << 20
        ),
        name="retro_block",
    )(jnp.transpose(nbr_index, (0, 2, 1)), seq_lengths, dec_query, dec_key, dec_value, cross_query, enc_query, enc_key, enc_value)
    return pl.pallas_call(
        place,
        out_shape=(shape, shape),
        in_specs=[any_] * 2,
        out_specs=(any_, any_),
        scratch_shapes=[V((4, 128, WIDTH), BF16), dma(4), dma(4)],
        name="place",
    )(*both)


def solution(mesh):
    rows = P("grp", "seq", "mp")
    store = P(("grp", "seq", "mp"), None, None)
    return jax.shard_map(
        local,
        mesh=mesh,
        in_specs=(rows, rows, rows, rows, store, store, store, P("grp", "seq", None), P("grp")),
        out_specs=(rows, rows),
        check_vma=False,
    )
```
